128 devices in a mesh: grp: 4 (over y_hi, core), gx: 8 (over z, y_lo), gy: 4 (over x).
Axes of the slice: x: 4, y: 4 (y_hi: 2, y_lo: 2; y = y_hi * 2 + y_lo), z: 4, core: 2. Of those that a mesh axis runs over, the one named last changes fastest.
Arguments:
- fields: float32 [4, 5, 128, 128, 384], P('grp', None, 'gx', 'gy'), may hold values from -6 to 6
- closure_in: float32 [64, 5], replicated, may hold values from -2.5 to 2.5
- closure_bias: float32 [64], replicated, may hold values from -4 to 4
- closure_out: float32 [64], replicated, may hold values from -0.75 to 0.75
- master: float32 [17280], replicated, may hold values from -0.6 to 0.6
- momentum: float32 [17280], replicated, may hold values from -3 to 3
- sample_block: int32 [96], replicated, may hold values from 0 to 47
- sample_trainer: int32 [96], replicated, may hold values from 0 to 31, as said below
Outputs:
- new_fields: float32 [4, 5, 128, 128, 384], P('grp', None, 'gx', 'gy')
- new_master: float32 [17280], P(('grp', 'gx', 'gy'))
- new_momentum: float32 [17280], P(('grp', 'gx', 'gy'))
The draws below stay inside these ranges and needn't reach their ends.
Inputs may be any that keep to these rules, and one draw needn't show every extreme that they name: `sample_trainer`: entry o names the trainer c = gx * 4 + gy of the last group that receives the cube of evolution device o. Every trainer receives at least 2 and at most 6 cubes, at most 4 from one evolution group; in every draw some trainer receives 6, 4 of them from one group.
All inputs are finite; a program needn't handle non-finite values.
Results may differ from the reference program's by a relative error of at most 0.0026.
The reference program's roundings to bfloat16 on the way (of `samples`, `hidden`, `error_grad` and `pre_grad`) count: a program that leaves them out, or rounds other values in their place, can miss the bound.
Values may be sent and summed in bfloat16 or wider, within the bound.
A program may use at most 192 MiB of HBM per device.

```python
import jax
import jax.numpy as jnp
from jax import lax

F = 5
CH = 64
HID = 64
SUB = 16
CX = 16
CY = 32
CZ = 384
TCAP = 6
INNER = 3
TRAINERS = 32
OWNERS = 96
NX = 128
NY = 128
CELLS = 4096
BLOCKS = 48
NPARAM = 17280
N_GRP = 4
N_GX = 8
N_GY = 4


def draw_master(key, part):
    first_count = CH * 27 * F
    position = jnp.arange(NPARAM)
    scales = jnp.where(position < first_count, (27.0 * F) ** (-0.5), (27.0 * CH) ** (-0.5))
    normal_draw = jax.random.truncated_normal(key, -6.0, 6.0, (NPARAM,), jnp.float32)
    return (normal_draw * scales).astype(jnp.float32)


def draw_sample_trainer(key, part):
    first_group = jax.random.permutation(jax.random.fold_in(key, 1), TRAINERS)
    busy_list = jax.random.permutation(jax.random.fold_in(key, 2), TRAINERS)
    spread = jax.random.permutation(jax.random.fold_in(key, 3), TRAINERS)
    third_group = jax.random.permutation(jax.random.fold_in(key, 4), TRAINERS)
    second_group = busy_list[spread // 4]
    return jnp.concatenate([first_group, second_group, third_group]).astype(jnp.int32)


def set_ends(values, key, smallest, high):
    longest = values.shape.index(max(values.shape))
    spots = []
    for shift in (0, 1):
        where = [jax.random.randint(jax.random.fold_in(key, axis), (), 0, length) for axis, length in enumerate(values.shape)]
        where[longest] = (where[longest] + shift) % values.shape[longest]
        spots.append(tuple(where))
    return values.at[spots[0]].set(smallest).at[spots[1]].set(high)


def steps_of(own_key, dims, pieces, least, top_value):
    loudness, own = 1.0, jax.random.fold_in(own_key, 6)
    for dim, shards_of in pieces:
        draws = jnp.exp(jax.random.uniform(jax.random.fold_in(own, dim), (shards_of,), jnp.float32, least / len(pieces), top_value / len(pieces)))
        loudness = loudness * jnp.repeat(draws, dims[dim] // shards_of).reshape([-1 if axis == dim else 1 for axis in range(len(dims))])
    return loudness


def bell_draw(stream_key, shape, width, reach, pieces=(), kind=jnp.bfloat16):
    loudness = steps_of(stream_key, shape, pieces, -0.22, 0.18) if pieces else 1.0
    drawn = jax.random.normal(stream_key, shape, jnp.float32) * width * loudness
    return jnp.minimum(jnp.maximum(drawn, -reach), reach).astype(kind)


def setup_inputs(seed: int = 0) -> dict:
    arg_keys = jax.random.split(jax.random.key(seed), 9)
    fields = bell_draw(arg_keys[0], (N_GRP, F, NX, NY, CZ), 1.0, 6.0, ((0, 4), (2, 8), (3, 4)), jnp.float32)
    closure_in = bell_draw(arg_keys[1], (HID, F), F ** -0.5, 2.5, (), jnp.float32)
    closure_bias = bell_draw(arg_keys[2], (HID,), 1.0, 4.0, (), jnp.float32)
    closure_out = bell_draw(arg_keys[3], (HID,), HID ** -0.5, 0.75, (), jnp.float32)
    master = draw_master(jax.random.fold_in(arg_keys[8], 71), 0)
    momentum = bell_draw(arg_keys[5], (NPARAM,), 0.5, 3.0, (), jnp.float32)
    sample_block = set_ends(jax.random.randint(arg_keys[6], (OWNERS,), 0, BLOCKS), jax.random.fold_in(arg_keys[6], 1), 0, BLOCKS - 1).astype(jnp.int32)
    sample_trainer = draw_sample_trainer(jax.random.fold_in(arg_keys[8], 71), 0)
    return {"fields": fields, "closure_in": closure_in, "closure_bias": closure_bias, "closure_out": closure_out, "master": master, "momentum": momentum, "sample_block": sample_block, "sample_trainer": sample_trainer}


time_step = 0.1
base_viscosity = 0.02
viscosity_gain = 0.2
buoyancy = 0.5
inner_rate = 0.02
outer_rate = 0.01
momentum_decay = 0.9
norm_epsilon = 1e-06
highest = lax.Precision.HIGHEST

def eddy_viscosity(center, closure_in, closure_bias, closure_out):
    channels, x_cells, y_cells, z_cells = center.shape
    flattened = center.reshape(channels, x_cells * y_cells * z_cells)
    block_size = 4 * y_cells * z_cells
    block_count = x_cells // 4

    def viscosity_block(block_index):
        columns = lax.dynamic_slice_in_dim(flattened, block_index * block_size, block_size, 1)
        hidden = jax.nn.silu(jnp.dot(closure_in, columns, precision=highest) + closure_bias[:, None])
        return viscosity_gain * jax.nn.softplus(jnp.dot(closure_out, hidden, precision=highest))
    blocks = lax.map(viscosity_block, jnp.arange(block_count, dtype=jnp.int32))
    return blocks.reshape(x_cells, y_cells, z_cells)

def field_tendency(padded, closure_in, closure_bias, closure_out):
    walled = jnp.pad(padded, ((0, 0), (0, 0), (0, 0), (1, 1)))
    center = walled[:, 1:-1, 1:-1, 1:-1]
    east_side = walled[:, 2:, 1:-1, 1:-1]
    west_side = walled[:, :-2, 1:-1, 1:-1]
    north_side = walled[:, 1:-1, 2:, 1:-1]
    south_side = walled[:, 1:-1, :-2, 1:-1]
    upper_side = walled[:, 1:-1, 1:-1, 2:]
    lower_side = walled[:, 1:-1, 1:-1, :-2]
    laplacian = east_side + west_side + north_side + south_side + upper_side + lower_side - 6.0 * center
    advection = center[0] * (east_side - west_side) + center[1] * (north_side - south_side) + center[2] * (upper_side - lower_side)
    viscosity = base_viscosity + eddy_viscosity(center, closure_in, closure_bias, closure_out)
    tendency = viscosity * laplacian - 0.5 * advection
    return tendency.at[2].add(buoyancy * center[3])

def shift_tables(edge_cells, slot_count):
    cube_cells = edge_cells * edge_cells * edge_cells
    position = jnp.arange(slot_count * cube_cells, dtype=jnp.int32) % cube_cells
    x_coord = position // (edge_cells * edge_cells)
    y_coord = position // edge_cells % edge_cells
    z_coord = position % edge_cells
    tables = []
    for x_step in (-1, 0, 1):
        for y_step in (-1, 0, 1):
            for z_step in (-1, 0, 1):
                offset = x_step * edge_cells * edge_cells + y_step * edge_cells + z_step
                inside = (x_coord + x_step >= 0) & (x_coord + x_step < edge_cells)
                inside = inside & (y_coord + y_step >= 0) & (y_coord + y_step < edge_cells)
                inside = inside & (z_coord + z_step >= 0) & (z_coord + z_step < edge_cells)
                tables.append((offset, inside))
    return tables

def shift_from(values, offset, inside):
    return jnp.where(inside, jnp.roll(values, -offset, axis=1), jnp.zeros((), values.dtype))

def shift_back(values, offset, inside):
    return jnp.roll(jnp.where(inside, values, jnp.zeros((), values.dtype)), offset, axis=1)

def stacked_from(values, tables):
    return jnp.concatenate([shift_from(values, offset, inside) for offset, inside in tables], axis=0)

def stacked_back(values, tables):
    return jnp.concatenate([shift_back(values, offset, inside) for offset, inside in tables], axis=0)

def silu_slope(values):
    sigmoid_value = jax.nn.sigmoid(values)
    return sigmoid_value * (1.0 + values * (1.0 - sigmoid_value))

def batch_gradient(flat_weights, inputs, targets, cell_weight, tables):
    first_count = CH * 27 * F
    first_weight = flat_weights[:first_count].reshape(CH, 27 * F)
    last_weight = flat_weights[first_count:].reshape(F, 27, CH)
    stacked_last = jnp.transpose(last_weight, (1, 0, 2)).reshape(27 * F, CH)
    input_stack = stacked_from(inputs, tables)
    first_pre = jnp.dot(first_weight, input_stack, preferred_element_type=jnp.float32)
    hidden = jax.nn.silu(first_pre).astype(jnp.bfloat16)
    partial_out = jnp.dot(stacked_last, hidden, preferred_element_type=jnp.float32)
    predicted = jnp.zeros((F, inputs.shape[1]), jnp.float32)
    for slot_index, (offset, inside) in enumerate(tables):
        predicted = predicted + shift_from(partial_out[slot_index * F:(slot_index + 1) * F], offset, inside)
    error_grad = (2.0 * cell_weight[None, :] * (predicted - targets.astype(jnp.float32))).astype(jnp.bfloat16)
    grad_stack = stacked_back(error_grad, tables)
    last_grad = lax.dot_general(grad_stack, hidden, (((1,), (1,)), ((), ())), preferred_element_type=jnp.float32)
    last_grad = jnp.transpose(last_grad.reshape(27, F, CH), (1, 0, 2)).reshape(F * 27 * CH)
    hidden_grad = lax.dot_general(stacked_last, grad_stack, (((0,), (0,)), ((), ())), preferred_element_type=jnp.float32)
    pre_grad = (hidden_grad * silu_slope(first_pre)).astype(jnp.bfloat16)
    first_grad = lax.dot_general(pre_grad, input_stack, (((1,), (1,)), ((), ())), preferred_element_type=jnp.float32)
    return jnp.concatenate([first_grad.reshape(CH * 27 * F), last_grad])

def local_train(flat_weights, inputs, targets, cell_weight, tables):
    start_weights = flat_weights.astype(jnp.float32)
    current = start_weights
    for inner_index in range(INNER):
        gradient = batch_gradient(current.astype(jnp.bfloat16), inputs, targets, cell_weight, tables)
        current = current - inner_rate * gradient
    return start_weights - current

def slot_lists(sample_trainer, trainers, column):
    owner_ids = jnp.arange(sample_trainer.shape[0], dtype=jnp.int32)
    same_trainer = sample_trainer[:, None] == sample_trainer[None, :]
    earlier = owner_ids[None, :] < owner_ids[:, None]
    rank_all = lax.optimization_barrier(jnp.sum((same_trainer & earlier).astype(jnp.int32), axis=1))
    mine_mask = sample_trainer == column
    slot_ids = jnp.arange(TCAP, dtype=jnp.int32)
    chosen = mine_mask[None, :] & (rank_all[None, :] == slot_ids[:, None])
    slot_owner = lax.optimization_barrier(jnp.sum(jnp.where(chosen, owner_ids[None, :], 0), axis=1)).astype(jnp.int32)
    slot_valid = jnp.any(chosen, axis=1)
    sample_count = jnp.maximum(jnp.sum(mine_mask.astype(jnp.int32)), 1)
    return (slot_owner, slot_valid, sample_count)

def train_batch(batch_cubes, slot_valid, sample_count, flat_weights, tables):
    inputs = jnp.transpose(batch_cubes[:, :F], (1, 0, 2)).reshape(F, TCAP * CELLS)
    targets = jnp.transpose(batch_cubes[:, F:], (1, 0, 2)).reshape(F, TCAP * CELLS)
    slot_weight = jnp.where(slot_valid, 1.0 / (sample_count.astype(jnp.float32) * CELLS), 0.0).astype(jnp.float32)
    cell_weight = jnp.repeat(slot_weight, CELLS)
    return local_train(flat_weights, inputs, targets, cell_weight, tables)

def reference(fields, closure_in, closure_bias, closure_out, master, momentum, sample_block, sample_trainer):
    trainers = N_GX * N_GY
    sim_groups = N_GRP - 1
    updated = []
    tendencies = []
    for group_index in range(sim_groups):
        slab_fields = fields[group_index]
        padded = jnp.pad(slab_fields, ((0, 0), (1, 1), (1, 1), (0, 0)), mode='wrap')
        tendency = field_tendency(padded, closure_in, closure_bias, closure_out)
        tendencies.append(tendency)
        updated.append(slab_fields + time_step * tendency)
    updated.append(fields[sim_groups])
    new_fields = jnp.stack(updated)
    tendency_all = jnp.stack(tendencies)
    y_blocks = CY // SUB
    z_blocks = CZ // SUB

    def cut_sample(owner_id):
        group_index = owner_id // trainers
        column = owner_id % trainers
        block_id = sample_block[owner_id]
        x_start = column // N_GY * CX + block_id // (y_blocks * z_blocks) * SUB
        y_start = column % N_GY * CY + block_id // z_blocks % y_blocks * SUB
        z_start = block_id % z_blocks * SUB
        corner = (group_index.astype(jnp.int32), jnp.int32(0), x_start.astype(jnp.int32), y_start.astype(jnp.int32), z_start.astype(jnp.int32))
        old_cube = lax.dynamic_slice(fields, corner, (1, F, SUB, SUB, SUB)).reshape(F, CELLS)
        new_cube = lax.dynamic_slice(tendency_all, corner, (1, F, SUB, SUB, SUB)).reshape(F, CELLS)
        return jnp.concatenate([old_cube.astype(jnp.bfloat16), new_cube.astype(jnp.bfloat16)], axis=0)
    samples = lax.map(cut_sample, jnp.arange(OWNERS, dtype=jnp.int32))
    tables = shift_tables(SUB, TCAP)
    flat_weights = master.astype(jnp.bfloat16)

    def trainer_delta(running, column):
        slot_owner, slot_valid, sample_count = slot_lists(sample_trainer, trainers, column)
        batch_cubes = jnp.where(slot_valid[:, None, None], jnp.take(samples, slot_owner, axis=0), jnp.zeros((), jnp.bfloat16))
        return (running + train_batch(batch_cubes, slot_valid, sample_count, flat_weights, tables), None)
    weight_delta, unused = lax.scan(trainer_delta, jnp.zeros((NPARAM,), jnp.float32), jnp.arange(trainers, dtype=jnp.int32))
    inverse = 1.0 / jnp.sqrt(jnp.sum(weight_delta * weight_delta) / NPARAM + norm_epsilon)
    new_momentum = momentum_decay * momentum + weight_delta * inverse
    new_master = master - outer_rate * new_momentum
    return (new_fields, new_master, new_momentum)
```

```python
import functools

import jax
import jax.numpy as jnp
from jax import lax
from jax.experimental import pallas as pl
from jax.experimental.pallas import tpu as pltpu
from jax.sharding import PartitionSpec as P

F = 5
CH = 64
SUB = 16
CX = 16
CY = 32
CZ = 384
TCAP = 6
INNER = 3
CELLS = 4096
NPARAM = 17280
FIRST = CH * 27 * F
KROWS = 240
BASE = 256
WIDE = CELLS + 2 * BASE
CHUNK = 512

time_step = 0.1
base_viscosity = 0.02
viscosity_gain = 0.2
buoyancy = 0.5
inner_rate = 0.02
outer_rate = 0.01
momentum_decay = 0.9
norm_epsilon = 1e-06
f32 = jnp.float32
bf16 = jnp.bfloat16
NT = (((1,), (1,)), ((), ()))


def iota(shape, dim):
    return lax.broadcasted_iota(jnp.int32, shape, dim)


def closure_table(closure_in, closure_bias):
    half = 0.5 * closure_in
    high = lax.reduce_precision(half, 8, 7)
    low = half - high
    bias = 0.5 * closure_bias
    bias_terms = []
    for _ in range(3):
        term = lax.reduce_precision(bias, 8, 7)
        bias_terms.append(term[:, None])
        bias = bias - term
    high = jnp.repeat(high, 16, axis=1)
    low = jnp.repeat(low, 16, axis=1)
    return jnp.concatenate([high, high, low] + bias_terms + [jnp.zeros((CH, 13), f32)], axis=1).astype(bf16)


def spread_closure(table_ref, wide_ref):
    for part in range(8):
        pick = (iota((128, CH), 0) // 16 + part * 8 == iota((128, CH), 1)).astype(f32).astype(bf16)
        rows = jnp.dot(pick, table_ref[...], preferred_element_type=f32)
        row = iota((128, 256), 0) % 16
        column = iota((128, 256), 1)
        keep = (row == column % 16) | (column >= 240)
        wide_ref[part * 128 : (part + 1) * 128, :] = jnp.where(keep, rows, 0.0).astype(bf16)


def closure(cells, wide_ref, out_ref):
    length = cells.shape[1]
    high = cells.astype(bf16)
    low = (cells - high.astype(f32)).astype(bf16)
    stack = jnp.concatenate([high, low, high, jnp.ones((16, length), bf16)], axis=0)
    total = jnp.zeros((16, length), f32)
    for part in range(8):
        half = jnp.dot(wide_ref[part * 128 : (part + 1) * 128, :], stack, preferred_element_type=f32)
        bent = jnp.tanh(half)
        for k in range(8):
            h = half[k * 16 : (k + 1) * 16]
            t = bent[k * 16 : (k + 1) * 16]
            total = total + out_ref[part * 8 + k] * (h + h * t)
    return viscosity_gain * (jnp.maximum(total, 0.0) + jnp.log1p(jnp.exp(-jnp.abs(total))))


def advance(center, east, west, north, south, upper, lower, eddy):
    viscosity = base_viscosity + eddy
    result = []
    for f in range(F):
        laplacian = east[f] + west[f] + north[f] + south[f] + upper[f] + lower[f] - 6.0 * center[f]
        advection = (
            center[0] * (east[f] - west[f])
            + center[1] * (north[f] - south[f])
            + center[2] * (upper[f] - lower[f])
        )
        value = viscosity * laplacian - 0.5 * advection
        if f == 2:
            value = value + buoyancy * center[3]
        result.append(value)
    return result


def cube_kernel(
    where_ref, out_ref, brick, x_low, x_high, y_low, y_high, table_ref, payload, wide_ref, window, north_rows, south_rows
):
    spread_closure(table_ref, wide_ref)
    y_half = where_ref[0]
    z_block = where_ref[1]
    y_start = pl.multiple_of(y_half * 16, 16)
    turn = lax.rem(CZ + 1 - z_block * 16, CZ)

    def cut(rows):
        rolled = pltpu.roll(rows, turn, 1)[:, :128]
        lane = iota(rolled.shape, 1)
        outside = ((lane == 0) & (z_block == 0)) | ((lane == 17) & (z_block == 23))
        return jnp.where(outside, 0.0, rolled)

    upper_half = y_half == 1
    for f in range(F):
        window[f, 0] = cut(x_low[f, pl.ds(y_start, 16), :])
        window[f, 17] = cut(x_high[f, pl.ds(y_start, 16), :])
        south_rows[f] = cut(jnp.where(upper_half, brick[f, :, 15, :], y_low[f]))
        north_rows[f] = cut(jnp.where(upper_half, y_high[f], brick[f, :, 16, :]))

    def load(x, carry):
        for f in range(F):
            window[f, x + 1] = cut(brick[f, x, pl.ds(y_start, 16), :])
        return carry

    lax.fori_loop(0, CX, load, 0, unroll=2)

    lane = iota((128, 256), 0)
    place = iota((128, 256), 1)
    unfold = (lane - 1 == place % 16).astype(f32).astype(bf16)
    own_row = iota((160, 256), 0) % 16 == iota((160, 256), 1) // 16
    group = iota((16, 160), 1) // 16
    gather = (jnp.where(group < 5, group, group + 3) == iota((16, 160), 0)).astype(f32).astype(bf16)
    row = iota((16, 128), 0)

    def quarter(i, carry):
        x0 = i * 4
        cells = jnp.concatenate(
            [
                jnp.concatenate([window[f, x0 + j + 1] for f in range(F)], axis=0)
                for j in range(4)
            ],
            axis=1,
        )
        eddies = closure(cells, wide_ref, out_ref)
        for j in range(4):
            x = x0 + j
            center = [window[f, x + 1] for f in range(F)]
            east = [window[f, x + 2] for f in range(F)]
            west = [window[f, x] for f in range(F)]
            north = [
                jnp.where(row == 15, north_rows[f, pl.ds(x, 1), :], pltpu.roll(center[f], 15, 0)) for f in range(F)
            ]
            south = [
                jnp.where(row == 0, south_rows[f, pl.ds(x, 1), :], pltpu.roll(center[f], 1, 0)) for f in range(F)
            ]
            upper = [pltpu.roll(center[f], 127, 1) for f in range(F)]
            lower = [pltpu.roll(center[f], 1, 1) for f in range(F)]
            tendency = advance(
                center, east, west, north, south, upper, lower, eddies[:, j * 128 : (j + 1) * 128]
            )
            both = jnp.concatenate(center + tendency, axis=0).astype(bf16)
            flat = jnp.dot(both, unfold, preferred_element_type=f32)
            flat = jnp.where(own_row, flat, 0.0).astype(bf16)
            flat = jnp.dot(gather, flat, preferred_element_type=f32).astype(bf16)
            payload[:, pl.ds(pl.multiple_of(x * 256, 256), 256)] = flat
        return carry

    lax.fori_loop(0, 4, quarter, 0)


def cube_call(where, closure_out, brick, x_low, x_high, y_low, y_high, table):
    smem = pl.BlockSpec(memory_space=pltpu.SMEM)
    vmem = pl.BlockSpec(memory_space=pltpu.VMEM)
    return pl.pallas_call(
        cube_kernel,
        out_shape=jax.ShapeDtypeStruct((16, CELLS), bf16),
        in_specs=[smem, smem] + [vmem] * 6,
        out_specs=vmem,
        scratch_shapes=[
            pltpu.VMEM((1024, 256), bf16),
            pltpu.VMEM((F, 18, 16, 128), f32),
            pltpu.VMEM((F, 16, 128), f32),
            pltpu.VMEM((F, 16, 128), f32),
        ],
        compiler_params=pltpu.CompilerParams(vmem_limit_bytes=40 * 2**20),
    )(where, closure_out, brick, x_low, x_high, y_low, y_high, table)


def evolve(out_ref, brick, x_low, x_high, y_low, y_high, table_ref, new_fields, wide_ref, padded, fresh, sems):
    copies = [
        pltpu.make_async_copy(brick, padded.at[:, pl.ds(1, CX)], sems.at[0]),
        pltpu.make_async_copy(x_low, padded.at[:, 0], sems.at[1]),
        pltpu.make_async_copy(x_high, padded.at[:, CX + 1], sems.at[2]),
    ]
    for copy in copies:
        copy.start()
    spread_closure(table_ref, wide_ref)
    for copy in copies:
        copy.wait()
    row = iota((CY, CZ), 0)
    lane = iota((CY, CZ), 1)

    def plane(x, carry):
        center = [padded[f, x + 1] for f in range(F)]
        cells = jnp.concatenate(
            [jnp.concatenate([c[h * 16 : (h + 1) * 16] for c in center], axis=0) for h in range(2)], axis=1
        )
        eddy = closure(cells, wide_ref, out_ref)
        eddy = jnp.concatenate([eddy[:, :CZ], eddy[:, CZ:]], axis=0)
        center = [padded[f, x + 1] for f in range(F)]
        east = [padded[f, x + 2] for f in range(F)]
        west = [padded[f, x] for f in range(F)]
        north = [
            jnp.where(row == CY - 1, y_high[f, pl.ds(x, 1), :], pltpu.roll(center[f], CY - 1, 0)) for f in range(F)
        ]
        south = [jnp.where(row == 0, y_low[f, pl.ds(x, 1), :], pltpu.roll(center[f], 1, 0)) for f in range(F)]
        upper = [jnp.where(lane == CZ - 1, 0.0, pltpu.roll(center[f], CZ - 1, 1)) for f in range(F)]
        lower = [jnp.where(lane == 0, 0.0, pltpu.roll(center[f], 1, 1)) for f in range(F)]
        tendency = advance(center, east, west, north, south, upper, lower, eddy)
        for f in range(F):
            fresh[f, x] = center[f] + time_step * tendency[f]
        pltpu.make_async_copy(fresh.at[:, x], new_fields.at[:, x], sems.at[3]).start()
        return carry

    lax.fori_loop(0, CX, plane, 0)
    pltpu.make_async_copy(fresh, new_fields, sems.at[3]).wait()


def shifted(values, y_step, z_step):
    length = values.shape[1]
    offset = 16 * y_step + z_step
    place = iota(values.shape, 1)
    if y_step:
        y = place // 16 % 16 + y_step
        inside = (y >= 0) & (y < 16)
    else:
        z = place % 16 + z_step
        inside = (z >= 0) & (z < 16)
    return jnp.where(inside, pltpu.roll(values, -offset % length, 1), 0.0)


STEPS = (-1, 0, 1)


def nine(values, sign):
    along_z = {s: values if s == 0 else shifted(values, 0, sign * s) for s in STEPS}
    rows = []
    for y_step in STEPS:
        for z_step in STEPS:
            part = along_z[z_step]
            rows.append(part if y_step == 0 else shifted(part, sign * y_step, 0))
    rows.append(jnp.zeros_like(values))
    return jnp.concatenate(rows, axis=0)


def train(scale_ref, cubes, start, delta, stacks, hiddens, slopes, errors, pres, now_first, now_last, now_out, grads):
    chunks = CELLS // CHUNK
    for x_step in STEPS:
        edge = slice(BASE, 2 * BASE) if x_step < 0 else slice(CELLS, CELLS + BASE)
        if x_step:
            block = x_step + 1
            empty = slice(BASE, 2 * BASE) if x_step > 0 else slice(CELLS, CELLS + BASE)
            errors[block * 80 : (block + 1) * 80, empty] = jnp.zeros((80, BASE), bf16)
            hiddens[block * CH : (block + 1) * CH, edge] = jnp.zeros((CH, BASE), bf16)
            for s in range(TCAP):
                stacks[s, block * 80 : (block + 1) * 80, edge] = jnp.zeros((80, BASE), bf16)

    def build(s, carry):
        for i in range(chunks):
            o = i * CHUNK
            values = cubes[s, :, o : o + CHUNK].astype(f32)[:8]
            rows = nine(values, 1).astype(bf16)
            for x_step in STEPS:
                at = BASE + o - BASE * x_step
                stacks[s, (x_step + 1) * 80 : (x_step + 2) * 80, at : at + CHUNK] = rows
        return carry

    lax.fori_loop(0, TCAP, build, 0)
    delta[...] = jnp.zeros_like(delta)
    eye = (iota((KROWS, KROWS), 0) == iota((KROWS, KROWS), 1)).astype(f32).astype(bf16)

    def step(k, carry):
        first = (start[0] - delta[0])[:, :KROWS].astype(bf16)
        last = (start[1] - delta[1])[:, :KROWS].astype(bf16)
        now_first[...] = first
        now_last[...] = last
        turned = lax.dot_general(eye, last, NT, preferred_element_type=f32)
        now_out[...] = jnp.concatenate([turned[b * 80 : (b + 1) * 80] for b in range(3)], axis=1).astype(bf16)
        grads[...] = jnp.zeros_like(grads)

        def cube(s, carry):
            scale = scale_ref[s]
            for i in range(chunks):
                o = BASE + i * CHUNK
                pre = jnp.dot(now_first[...], stacks[s, :, o : o + CHUNK], preferred_element_type=f32)
                sigmoid = 0.5 + 0.5 * jnp.tanh(0.5 * pre)
                hidden = pre * sigmoid
                slopes[:, i * CHUNK : (i + 1) * CHUNK] = sigmoid + hidden * (1.0 - sigmoid)
                hidden = hidden.astype(bf16)
                for x_step in STEPS:
                    at = o - BASE * x_step
                    hiddens[(x_step + 1) * CH : (x_step + 2) * CH, at : at + CHUNK] = hidden
            for i in range(chunks):
                o = BASE + i * CHUNK
                parts = jnp.dot(now_out[...], hiddens[:, o : o + CHUNK], preferred_element_type=f32)
                predicted = None
                for z_step in STEPS:
                    line = None
                    for y_step in STEPS:
                        row = ((y_step + 1) * 3 + z_step + 1) * 8
                        part = parts[row : row + 8]
                        part = part if y_step == 0 else shifted(part, y_step, 0)
                        line = part if line is None else line + part
                    line = line if z_step == 0 else shifted(line, 0, z_step)
                    predicted = line if predicted is None else predicted + line
                targets = cubes[s, :, i * CHUNK : (i + 1) * CHUNK].astype(f32)[8:]
                error = (scale * (predicted - targets)).astype(bf16).astype(f32)
                rows = nine(error, -1).astype(bf16)
                for x_step in STEPS:
                    at = o + BASE * x_step
                    errors[(x_step + 1) * 80 : (x_step + 2) * 80, at : at + CHUNK] = rows
            for i in range(chunks):
                o = BASE + i * CHUNK
                back = jnp.dot(
                    now_last[...], errors[:, o : o + CHUNK], preferred_element_type=f32
                )
                pres[:, i * CHUNK : (i + 1) * CHUNK] = (back * slopes[:, i * CHUNK : (i + 1) * CHUNK]).astype(bf16)
            cells = slice(BASE, BASE + CELLS)
            grads[0] += lax.dot_general(pres[...], stacks[s, :, cells], NT, preferred_element_type=f32)
            grads[1] += lax.dot_general(
                hiddens[CH : 2 * CH, cells], errors[:, cells], NT, preferred_element_type=f32
            )
            return carry

        lax.fori_loop(0, TCAP, cube, 0)
        delta[:, :, :KROWS] += inner_rate * grads[...]
        return carry

    lax.fori_loop(0, INNER, step, 0)


def work_kernel(
    scale_ref, out_ref, cubes, start, table_ref, y_low, y_high, brick, x_low, x_high,
    new_fields, delta,
    wide_ref, padded, fresh, stacks, hiddens, slopes, errors, pres, now_first, now_last, now_out, grads, sems,
):
    is_trainer = lax.axis_index("grp") == lax.axis_size("grp") - 1

    @pl.when(is_trainer)
    def _():
        copy = pltpu.make_async_copy(brick, new_fields, sems.at[0])
        copy.start()
        train(
            scale_ref, cubes, start, delta, stacks, hiddens, slopes, errors, pres, now_first, now_last, now_out, grads
        )
        copy.wait()

    @pl.when(jnp.logical_not(is_trainer))
    def _():
        delta[...] = jnp.zeros_like(delta)
        evolve(out_ref, brick, x_low, x_high, y_low, y_high, table_ref, new_fields, wide_ref, padded, fresh, sems)


def work_call(scale, closure_out, cubes, start, table, y_low, y_high, brick, x_low, x_high):
    smem = pl.BlockSpec(memory_space=pltpu.SMEM)
    vmem = pl.BlockSpec(memory_space=pltpu.VMEM)
    anywhere = pl.BlockSpec(memory_space=pl.ANY)
    return pl.pallas_call(
        work_kernel,
        out_shape=(
            jax.ShapeDtypeStruct((F, CX, CY, CZ), f32),
            jax.ShapeDtypeStruct((2, CH, 256), f32),
        ),
        in_specs=[smem, smem, vmem, vmem, vmem, vmem, vmem, anywhere, anywhere, anywhere],
        out_specs=(anywhere, vmem),
        scratch_shapes=[
            pltpu.VMEM((1024, 256), bf16),
            pltpu.VMEM((F, CX + 2, CY, CZ), f32),
            pltpu.VMEM((F, CX, CY, CZ), f32),
            pltpu.VMEM((TCAP, KROWS, WIDE), bf16),
            pltpu.VMEM((3 * CH, WIDE), bf16),
            pltpu.VMEM((CH, CELLS), f32),
            pltpu.VMEM((KROWS, WIDE), bf16),
            pltpu.VMEM((CH, CELLS), bf16),
            pltpu.VMEM((CH, KROWS), bf16),
            pltpu.VMEM((CH, KROWS), bf16),
            pltpu.VMEM((80, 3 * CH), bf16),
            pltpu.VMEM((2, CH, KROWS), f32),
            pltpu.SemaphoreType.DMA((4,)),
        ],
        compiler_params=pltpu.CompilerParams(vmem_limit_bytes=56 * 2**20),
    )(scale, closure_out, cubes, start, table, y_low, y_high, brick, x_low, x_high)


def to_tables(flat):
    first = flat[:FIRST].reshape(CH, 3, 9, F)
    last = jnp.transpose(flat[FIRST:].reshape(F, 3, 9, CH), (3, 1, 2, 0))
    both = jnp.stack([first, last])
    both = jnp.pad(both, ((0, 0), (0, 0), (0, 0), (0, 1), (0, 3))).reshape(2, CH, KROWS)
    return jnp.pad(both, ((0, 0), (0, 0), (0, 256 - KROWS)))


def from_tables(both):
    both = both[:, :, :KROWS].reshape(2, CH, 3, 10, 8)[:, :, :, :9, :F]
    first = both[0].reshape(FIRST)
    last = jnp.transpose(both[1], (3, 1, 2, 0)).reshape(FIRST)
    return jnp.concatenate([first, last])


def slot_lists(sample_trainer, column):
    owner_ids = jnp.arange(sample_trainer.shape[0], dtype=jnp.int32)
    same_trainer = sample_trainer[:, None] == sample_trainer[None, :]
    earlier = owner_ids[None, :] < owner_ids[:, None]
    rank_all = jnp.sum((same_trainer & earlier).astype(jnp.int32), axis=1)
    mine_mask = sample_trainer == column
    slot_ids = jnp.arange(TCAP, dtype=jnp.int32)
    chosen = mine_mask[None, :] & (rank_all[None, :] == slot_ids[:, None])
    slot_owner = jnp.sum(jnp.where(chosen, owner_ids[None, :], 0), axis=1)
    slot_valid = jnp.any(chosen, axis=1)
    sample_count = jnp.maximum(jnp.sum(mine_mask.astype(jnp.int32)), 1)
    return (slot_owner, slot_valid, sample_count)


def neighbours(face_low, face_high, axis):
    count = lax.axis_size(axis)
    up = [(i, (i + 1) % count) for i in range(count)]
    down = [((i + 1) % count, i) for i in range(count)]
    return lax.ppermute(face_high, axis, up), lax.ppermute(face_low, axis, down)


def on_device(
    fields, closure_in, closure_bias, closure_out, master, momentum, sample_block, sample_trainer
):
    group_count = lax.axis_size("grp")
    y_devices = lax.axis_size("gy")
    trainers = lax.axis_size("gx") * y_devices
    my_group = lax.axis_index("grp")
    my_column = lax.axis_index("gx") * y_devices + lax.axis_index("gy")
    brick = fields[0]
    x_low, x_high = neighbours(brick[:, 0], brick[:, CX - 1], "gx")
    y_low, y_high = neighbours(brick[:, :, 0], brick[:, :, CY - 1], "gy")
    table = closure_table(closure_in, closure_bias)
    start = to_tables(lax.reduce_precision(master, 8, 7))

    sim_group = jnp.minimum(my_group, group_count - 2)
    block_id = sample_block[sim_group * trainers + my_column]
    where = jnp.stack([block_id // 24, block_id % 24])
    payload = cube_call(where, closure_out, brick, x_low, x_high, y_low, y_high, table)
    arrived = lax.all_gather(payload, ("grp", "gx", "gy"))
    slot_owner, slot_valid, sample_count = slot_lists(sample_trainer, my_column)
    cubes = jnp.stack(
        [lax.dynamic_index_in_dim(arrived, slot_owner[s], 0, keepdims=False) for s in range(TCAP)]
    )
    cubes = jnp.where(slot_valid[:, None, None], cubes, jnp.zeros((), bf16))
    scale = 2.0 * jnp.where(slot_valid, 1.0 / (sample_count.astype(f32) * CELLS), 0.0)
    new_fields, delta = work_call(
        scale, closure_out, cubes, start, table, y_low, y_high, brick, x_low, x_high
    )

    total_delta = from_tables(lax.psum(delta, ("grp", "gx", "gy")))
    share_size = NPARAM // (group_count * trainers)
    share_start = (my_group * trainers + my_column) * share_size
    momentum_share = lax.dynamic_slice_in_dim(momentum, share_start, share_size)
    master_share = lax.dynamic_slice_in_dim(master, share_start, share_size)
    inverse = 1.0 / jnp.sqrt(jnp.sum(total_delta * total_delta) / NPARAM + norm_epsilon)
    delta_share = lax.dynamic_slice_in_dim(total_delta, share_start, share_size)
    new_momentum = momentum_decay * momentum_share + delta_share * inverse
    new_master = master_share - outer_rate * new_momentum
    return (new_fields[None], new_master, new_momentum)


def solution(mesh):
    in_specs = (P("grp", None, "gx", "gy", None), P(), P(), P(), P(), P(), P(), P())
    out_specs = (P("grp", None, "gx", "gy", None), P(("grp", "gx", "gy")), P(("grp", "gx", "gy")))
    return jax.shard_map(
        on_device, mesh=mesh, in_specs=in_specs, out_specs=out_specs, check_vma=False
    )
```

```python
import jax
import jax.numpy as jnp
from jax import lax
from jax.experimental import pallas as pl
from jax.experimental.pallas import tpu as pltpu
from jax.sharding import PartitionSpec as P

F = 5
CH = 64
SUB = 16
CX = 16
CY = 32
CZ = 384
INNER = 3
CELLS = 4096
NPARAM = 17280
FIRST = CH * 27 * F
OWNERS = 96
TRAINERS = 32
TILES = 32
KROWS = 240
BASE = 256
WIDE = CELLS + 2 * BASE
CHUNK = 512

time_step = 0.1
base_viscosity = 0.02
viscosity_gain = 0.2
buoyancy = 0.5
inner_rate = 0.02
outer_rate = 0.01
momentum_decay = 0.9
norm_epsilon = 1e-06
f32 = jnp.float32
bf16 = jnp.bfloat16
NT = (((1,), (1,)), ((), ()))


def iota(shape, dim):
    return lax.broadcasted_iota(jnp.int32, shape, dim)


def spread_closure(closure_in, closure_bias, wide_ref):
    half = 0.5 * closure_in[...]
    high = half.astype(bf16)
    low = (half - high.astype(f32)).astype(bf16)
    column = iota((F, 256), 1)
    fields = (iota((F, 256), 0) == column // 16 % F) & (column < 240)
    of_high = (fields & (column < 160)).astype(f32).astype(bf16)
    of_low = (fields & (column >= 160)).astype(f32).astype(bf16)
    table = jnp.dot(high, of_high, preferred_element_type=f32) + jnp.dot(low, of_low, preferred_element_type=f32)
    diagonal = iota((CH, CH), 0) == iota((CH, CH), 1)
    bias = 0.5 * jnp.sum(jnp.where(diagonal, closure_bias[...], 0.0), axis=1, keepdims=True)
    lane = iota((CH, 256), 1)
    for place in range(240, 243):
        term = bias.astype(bf16).astype(f32)
        table = jnp.where(lane == place, term, table)
        bias = bias - term
    table = table.astype(bf16)
    for part in range(8):
        pick = (iota((128, CH), 0) // 16 + part * 8 == iota((128, CH), 1)).astype(f32).astype(bf16)
        rows = jnp.dot(pick, table, preferred_element_type=f32)
        row = iota((128, 256), 0) % 16
        column = iota((128, 256), 1)
        keep = (row == column % 16) | (column >= 240)
        wide_ref[part * 128 : (part + 1) * 128, :] = jnp.where(keep, rows, 0.0).astype(bf16)


def closure(cells, wide_ref, out_ref):
    length = cells.shape[1]
    high = cells.astype(bf16)
    low = (cells - high.astype(f32)).astype(bf16)
    stack = jnp.concatenate([high, low, high, jnp.ones((16, length), bf16)], axis=0)
    total = jnp.zeros((16, length), f32)
    for part in range(8):
        half = jnp.dot(wide_ref[part * 128 : (part + 1) * 128, :], stack, preferred_element_type=f32)
        bent = jnp.tanh(half)
        for k in range(8):
            h = half[k * 16 : (k + 1) * 16]
            t = bent[k * 16 : (k + 1) * 16]
            total = total + out_ref[part * 8 + k] * (h + h * t)
    return viscosity_gain * (jnp.maximum(total, 0.0) + jnp.log1p(jnp.exp(-jnp.abs(total))))


def advance(center, east, west, north, south, upper, lower, eddy):
    viscosity = base_viscosity + eddy
    result = []
    for f in range(F):
        laplacian = east[f] + west[f] + north[f] + south[f] + upper[f] + lower[f] - 6.0 * center[f]
        advection = (
            center[0] * (east[f] - west[f])
            + center[1] * (north[f] - south[f])
            + center[2] * (upper[f] - lower[f])
        )
        value = viscosity * laplacian - 0.5 * advection
        if f == 2:
            value = value + buoyancy * center[3]
        result.append(value)
    return result


def cut_cube(block, out_ref, padded, y_low, y_high, payload, wide_ref, window, north_rows, south_rows):
    upper_half = block // 24 == 1
    z_block = block % 24
    turn = lax.rem(CZ + 1 - z_block * 16, CZ)

    def cut(rows):
        rolled = pltpu.roll(rows, turn, 1)[:, :128]
        lane = iota(rolled.shape, 1)
        outside = ((lane == 0) & (z_block == 0)) | ((lane == 17) & (z_block == 23))
        return jnp.where(outside, 0.0, rolled)

    for f in range(F):
        south_rows[f] = cut(jnp.where(upper_half, padded[f, 1 : CX + 1, 15, :], y_low[f]))
        north_rows[f] = cut(jnp.where(upper_half, y_high[f], padded[f, 1 : CX + 1, 16, :]))

    def load(x, carry):
        for f in range(F):
            window[f, x] = cut(jnp.where(upper_half, padded[f, x, 16:, :], padded[f, x, :16, :]))
        return carry

    lax.fori_loop(0, CX + 2, load, 0, unroll=2)

    lane = iota((128, 256), 0)
    place = iota((128, 256), 1)
    unfold = (lane - 1 == place % 16).astype(f32).astype(bf16)
    own_row = iota((160, 256), 0) % 16 == iota((160, 256), 1) // 16
    group = iota((16, 160), 1) // 16
    gather = (jnp.where(group < 5, group, group + 3) == iota((16, 160), 0)).astype(f32).astype(bf16)
    row = iota((16, 128), 0)

    def quarter(i, carry):
        x0 = i * 4
        cells = jnp.concatenate(
            [jnp.concatenate([window[f, x0 + j + 1] for f in range(F)], axis=0) for j in range(4)], axis=1
        )
        eddies = closure(cells, wide_ref, out_ref)
        for j in range(4):
            x = x0 + j
            center = [window[f, x + 1] for f in range(F)]
            east = [window[f, x + 2] for f in range(F)]
            west = [window[f, x] for f in range(F)]
            north = [
                jnp.where(row == 15, north_rows[f, pl.ds(x, 1), :], pltpu.roll(center[f], 15, 0)) for f in range(F)
            ]
            south = [
                jnp.where(row == 0, south_rows[f, pl.ds(x, 1), :], pltpu.roll(center[f], 1, 0)) for f in range(F)
            ]
            upper = [pltpu.roll(center[f], 127, 1) for f in range(F)]
            lower = [pltpu.roll(center[f], 1, 1) for f in range(F)]
            tendency = advance(
                center, east, west, north, south, upper, lower, eddies[:, j * 128 : (j + 1) * 128]
            )
            both = jnp.concatenate(center + tendency, axis=0).astype(bf16)
            flat = jnp.dot(both, unfold, preferred_element_type=f32)
            flat = jnp.where(own_row, flat, 0.0).astype(bf16)
            flat = jnp.dot(gather, flat, preferred_element_type=f32).astype(bf16)
            payload[:, pl.ds(pl.multiple_of(x * 256, 256), 256)] = flat
        return carry

    lax.fori_loop(0, 4, quarter, 0)


def evolve(begin, end, out_ref, padded, y_low, y_high, new_fields, wide_ref, fresh, sem):
    row = iota((CY, CZ), 0)
    lane = iota((CY, CZ), 1)

    def plane(x, carry):
        center = [padded[f, x + 1] for f in range(F)]
        cells = jnp.concatenate(
            [jnp.concatenate([c[h * 16 : (h + 1) * 16] for c in center], axis=0) for h in range(2)], axis=1
        )
        eddy = closure(cells, wide_ref, out_ref)
        eddy = jnp.concatenate([eddy[:, :CZ], eddy[:, CZ:]], axis=0)
        center = [padded[f, x + 1] for f in range(F)]
        east = [padded[f, x + 2] for f in range(F)]
        west = [padded[f, x] for f in range(F)]
        north = [
            jnp.where(row == CY - 1, y_high[f, pl.ds(x, 1), :], pltpu.roll(center[f], CY - 1, 0)) for f in range(F)
        ]
        south = [jnp.where(row == 0, y_low[f, pl.ds(x, 1), :], pltpu.roll(center[f], 1, 0)) for f in range(F)]
        upper = [jnp.where(lane == CZ - 1, 0.0, pltpu.roll(center[f], CZ - 1, 1)) for f in range(F)]
        lower = [jnp.where(lane == 0, 0.0, pltpu.roll(center[f], 1, 1)) for f in range(F)]
        tendency = advance(center, east, west, north, south, upper, lower, eddy)
        for f in range(F):
            fresh[f, x] = center[f] + time_step * tendency[f]
        return carry

    lax.fori_loop(begin, end, plane, 0)
    copy = pltpu.make_async_copy(
        fresh.at[:, pl.ds(begin, end - begin)], new_fields.at[:, pl.ds(begin, end - begin)], sem
    )
    copy.start()
    return copy


def shifted(values, y_step, z_step):
    length = values.shape[1]
    offset = 16 * y_step + z_step
    place = iota(values.shape, 1)
    if y_step:
        y = place // 16 % 16 + y_step
        inside = (y >= 0) & (y < 16)
    else:
        z = place % 16 + z_step
        inside = (z >= 0) & (z < 16)
    return jnp.where(inside, pltpu.roll(values, -offset % length, 1), 0.0)


STEPS = (-1, 0, 1)


def nine(values, sign):
    along_z = {s: values if s == 0 else shifted(values, 0, sign * s) for s in STEPS}
    rows = []
    for y_step in STEPS:
        for z_step in STEPS:
            part = along_z[z_step]
            rows.append(part if y_step == 0 else shifted(part, sign * y_step, 0))
    rows.append(jnp.zeros_like(values))
    return jnp.concatenate(rows, axis=0)


def build_stack(payload, stack, hiddens, errors):
    for x_step in STEPS:
        if x_step:
            block = x_step + 1
            ends = (slice(BASE, 2 * BASE), slice(CELLS, CELLS + BASE))
            edge, empty = ends if x_step < 0 else ends[::-1]
            errors[block * 80 : (block + 1) * 80, empty] = jnp.zeros((80, BASE), bf16)
            hiddens[block * CH : (block + 1) * CH, edge] = jnp.zeros((CH, BASE), bf16)
            stack[block * 80 : (block + 1) * 80, edge] = jnp.zeros((80, BASE), bf16)
    for o in range(0, CELLS, CHUNK):
        rows = nine(payload[:, o : o + CHUNK].astype(f32)[:8], 1).astype(bf16)
        for x_step in STEPS:
            at = BASE + o - BASE * x_step
            stack[(x_step + 1) * 80 : (x_step + 2) * 80, at : at + CHUNK] = rows


def table_of(tiles, layer):
    return jnp.concatenate(
        [tiles[layer * 128 : layer * 128 + 64, :], tiles[layer * 128 + 64 : layer * 128 + 128, :]], axis=1
    )


def set_table(tiles, layer, table):
    tiles[layer * 128 : layer * 128 + 64, :] = table[:, :128]
    tiles[layer * 128 + 64 : layer * 128 + 128, :] = table[:, 128:]


def gradient(scale, weights, payload, stack, hiddens, slopes, errors, pres, now_first, now_last, now_out, grad):
    eye = (iota((KROWS, KROWS), 0) == iota((KROWS, KROWS), 1)).astype(f32).astype(bf16)
    now_first[...] = table_of(weights, 0)[:, :KROWS].astype(bf16)
    last = table_of(weights, 1)[:, :KROWS].astype(bf16)
    now_last[...] = last
    turned = lax.dot_general(eye, last, NT, preferred_element_type=f32)
    now_out[...] = jnp.concatenate([turned[b * 80 : (b + 1) * 80] for b in range(3)], axis=1).astype(bf16)
    for i in range(0, CELLS, CHUNK):
        o = BASE + i
        pre = jnp.dot(now_first[...], stack[:, o : o + CHUNK], preferred_element_type=f32)
        sigmoid = 0.5 + 0.5 * jnp.tanh(0.5 * pre)
        hidden = pre * sigmoid
        slopes[:, i : i + CHUNK] = sigmoid + hidden * (1.0 - sigmoid)
        hidden = hidden.astype(bf16)
        for x_step in STEPS:
            at = o - BASE * x_step
            hiddens[(x_step + 1) * CH : (x_step + 2) * CH, at : at + CHUNK] = hidden
    for i in range(0, CELLS, CHUNK):
        o = BASE + i
        parts = jnp.dot(now_out[...], hiddens[:, o : o + CHUNK], preferred_element_type=f32)
        predicted = None
        for z_step in STEPS:
            line = None
            for y_step in STEPS:
                row = ((y_step + 1) * 3 + z_step + 1) * 8
                part = parts[row : row + 8]
                part = part if y_step == 0 else shifted(part, y_step, 0)
                line = part if line is None else line + part
            line = line if z_step == 0 else shifted(line, 0, z_step)
            predicted = line if predicted is None else predicted + line
        targets = payload[:, i : i + CHUNK].astype(f32)[8:]
        error = (scale * (predicted - targets)).astype(bf16).astype(f32)
        rows = nine(error, -1).astype(bf16)
        for x_step in STEPS:
            at = o + BASE * x_step
            errors[(x_step + 1) * 80 : (x_step + 2) * 80, at : at + CHUNK] = rows
    for i in range(0, CELLS, CHUNK):
        o = BASE + i
        back = jnp.dot(now_last[...], errors[:, o : o + CHUNK], preferred_element_type=f32)
        pres[:, i : i + CHUNK] = (back * slopes[:, i : i + CHUNK]).astype(bf16)
    cells = slice(BASE, BASE + CELLS)
    spare = jnp.zeros((CH, 256 - KROWS), f32)
    first = lax.dot_general(pres[...], stack[:, cells], NT, preferred_element_type=f32)
    set_table(grad, 0, jnp.concatenate([first, spare], axis=1))
    last = lax.dot_general(hiddens[CH : 2 * CH, cells], errors[:, cells], NT, preferred_element_type=f32)
    set_table(grad, 1, jnp.concatenate([last, spare], axis=1))


def three_terms(values):
    high = values.astype(bf16)
    rest = values - high.astype(f32)
    middle = rest.astype(bf16)
    return high, middle, (rest - middle.astype(f32)).astype(bf16)


def places(layer):
    lane = iota((135, 256), 1)
    x_step, rest = lane // 80, lane % 80
    offset, field = x_step * 9 + rest // 8, rest % 8
    index = offset * F + field if layer == 0 else field * 27 + offset
    valid = (lane < KROWS) & (rest < 72) & (field < F)
    return (valid & (index == iota((135, 256), 0))).astype(f32).astype(bf16)


def device(group, column):
    columns = lax.axis_size("gy")
    return {"grp": group, "gx": column // columns, "gy": lax.rem(column, columns)}


def whole(ref, sem):
    return pltpu.make_async_copy(ref, ref, sem)


def step_kernel(
    block_ref, trainer_ref, out_ref, closure_in, closure_bias, trainer_row, first_in, last_in, brick,
    new_fields, first_out, last_out,
    wide_ref, padded, fresh, y_low, y_high, y_send, payload, window, north_rows, south_rows,
    stack, hiddens, slopes, errors, pres, now_first, now_last, now_out,
    start, weights, grad, gathered, answer, running, delta,
    load_sem, halo_send, halo_recv, store_sems, up_send, up_recv, down_send, down_recv, last_send, last_recv,
):
    group = lax.axis_index("grp")
    column = lax.axis_index("gx") * lax.axis_size("gy") + lax.axis_index("gy")
    me = group * TRAINERS + column
    last_group = lax.axis_size("grp") - 1

    def start_tables():
        table = jnp.dot(first_in[...].astype(bf16), places(0), preferred_element_type=f32)
        set_table(start, 0, table)
        table = lax.dot_general(
            last_in[...].astype(bf16), places(1), (((0,), (0,)), ((), ())), preferred_element_type=f32
        )
        set_table(start, 1, table)

    @pl.when(group < last_group)
    def _():
        load = pltpu.make_async_copy(brick, padded.at[:, pl.ds(1, CX)], load_sem)
        load.start()
        gx, gy = lax.axis_index("gx"), lax.axis_index("gy")
        gx_size, gy_size = lax.axis_size("gx"), lax.axis_size("gy")
        x_next, x_last = lax.rem(gx + 1, gx_size), lax.rem(gx + gx_size - 1, gx_size)
        y_next, y_last = lax.rem(gy + 1, gy_size), lax.rem(gy + gy_size - 1, gy_size)
        to_next_x = pltpu.make_async_remote_copy(
            brick.at[:, CX - 1], padded.at[:, 0], halo_send.at[0], halo_recv.at[0], device_id={"gx": x_next}
        )
        to_last_x = pltpu.make_async_remote_copy(
            brick.at[:, 0], padded.at[:, CX + 1], halo_send.at[1], halo_recv.at[1], device_id={"gx": x_last}
        )
        to_next_x.start()
        to_last_x.start()
        load.wait()
        for f in range(F):
            y_send[0, f] = padded[f, 1 : CX + 1, CY - 1, :]
            y_send[1, f] = padded[f, 1 : CX + 1, 0, :]
        to_next_y = pltpu.make_async_remote_copy(
            y_send.at[0], y_low, halo_send.at[2], halo_recv.at[2], device_id={"gy": y_next}
        )
        to_last_y = pltpu.make_async_remote_copy(
            y_send.at[1], y_high, halo_send.at[3], halo_recv.at[3], device_id={"gy": y_last}
        )
        to_next_y.start()
        to_last_y.start()
        spread_closure(closure_in, closure_bias, wide_ref)
        start_tables()
        same = (trainer_row[...] == trainer_ref[me]).astype(f32)
        count = jnp.sum(same, axis=1, keepdims=True)
        scale = 2.0 * (1.0 / (count * CELLS))
        for copy in (to_next_x, to_last_x, to_next_y, to_last_y):
            copy.wait()
        cut_cube(block_ref[me], out_ref, padded, y_low, y_high, payload, wide_ref, window, north_rows, south_rows)
        build_stack(payload, stack, hiddens, errors)
        bounds = (0, 5, 10, CX)
        stores = []
        for k in range(INNER):
            gradient(
                scale, weights if k else start, payload, stack, hiddens, slopes, errors, pres,
                now_first, now_last, now_out, grad,
            )

            def send(j, carry):
                to = lax.rem(column + j, TILES)
                pltpu.make_async_remote_copy(
                    grad.at[pl.ds(pl.multiple_of(to * 8, 8), 8)],
                    gathered.at[pl.ds(pl.multiple_of(me * 8, 8), 8)],
                    up_send,
                    up_recv,
                    device_id=device(last_group, to),
                ).start()
                return carry

            lax.fori_loop(0, TILES, send, 0, unroll=4)
            stores.append(
                evolve(
                    bounds[k], bounds[k + 1], out_ref, padded, y_low, y_high, new_fields, wide_ref, fresh,
                    store_sems.at[k],
                )
            )
            whole(grad, up_send).wait()
            if k < INNER - 1:
                whole(weights, down_recv).wait()
        for store in stores:
            store.wait()
        whole(delta, last_recv).wait()

    @pl.when(group == last_group)
    def _():
        keep = pltpu.make_async_copy(brick, new_fields, load_sem)
        keep.start()
        start_tables()
        own_start = start[pl.ds(pl.multiple_of(column * 8, 8), 8), :]
        square = (OWNERS, OWNERS)
        across = jnp.broadcast_to(trainer_row[...].astype(f32), square)
        diagonal = jnp.where(iota(square, 0) == iota(square, 1), across, 0.0)
        down = jnp.sum(diagonal, axis=1, keepdims=True)
        same = (across == down).astype(f32).astype(bf16)
        running[...] = jnp.zeros_like(running)
        total = jnp.zeros((8, 128), f32)
        for k in range(INNER):
            whole(gathered, up_recv).wait()

            def add(o, total):
                return total + gathered[pl.ds(pl.multiple_of(o * 8, 8), 8), :]

            total = lax.fori_loop(0, OWNERS, add, total, unroll=8)
            if k < INNER - 1:
                if k:
                    whole(answer, down_send).wait()
                for r in range(8):
                    terms = three_terms(gathered[pl.ds(r, OWNERS, stride=8), :])
                    part = sum(jnp.dot(same, term, preferred_element_type=f32) for term in terms)
                    part = running[r] + part
                    running[r] = part
                    answer[pl.ds(r, OWNERS, stride=8), :] = own_start[r : r + 1] - inner_rate * part

                def send(j, carry):
                    to = lax.rem(column + j, TRAINERS)
                    for g in range(OWNERS // TRAINERS):
                        pltpu.make_async_remote_copy(
                            answer.at[pl.ds(pl.multiple_of((g * TRAINERS + to) * 8, 8), 8)],
                            weights.at[pl.ds(pl.multiple_of(column * 8, 8), 8)],
                            down_send,
                            down_recv,
                            device_id=device(g, to),
                        ).start()
                    return carry

                lax.fori_loop(0, TRAINERS, send, 0, unroll=2)
        whole(answer, down_send).wait()
        own = delta.at[pl.ds(pl.multiple_of(column * 8, 8), 8)]
        own[...] = inner_rate * total

        def tell(j, carry):
            to = lax.rem(me + j, OWNERS + TRAINERS)
            pltpu.make_async_remote_copy(
                own, own, last_send, last_recv, device_id=device(to // TRAINERS, lax.rem(to, TRAINERS))
            ).start()
            return carry

        lax.fori_loop(1, OWNERS + TRAINERS, tell, 0)
        others = delta.at[pl.ds(0, (TILES - 1) * 8)]
        whole(others, last_recv).wait()
        for part in range(3):
            whole(delta, last_send).wait()
        whole(others, last_send).wait()
        keep.wait()

    values = delta[...]
    inverse = lax.rsqrt(jnp.sum(values * values) / NPARAM + norm_epsilon)
    first_out[...] = sum(
        lax.dot_general(term, places(0), NT, preferred_element_type=f32)
        for term in three_terms(table_of(delta, 0) * inverse)
    )
    last_out[...] = sum(
        lax.dot_general(places(1), term, NT, preferred_element_type=f32)
        for term in three_terms(table_of(delta, 1) * inverse)
    )


def step_call(sample_block, sample_trainer, closure_out, closure_in, closure_bias, first_in, last_in, brick):
    smem = pl.BlockSpec(memory_space=pltpu.SMEM)
    vmem = pl.BlockSpec(memory_space=pltpu.VMEM)
    anywhere = pl.BlockSpec(memory_space=pl.ANY)
    dma = pltpu.SemaphoreType.DMA
    return pl.pallas_call(
        step_kernel,
        out_shape=(
            jax.ShapeDtypeStruct((F, CX, CY, CZ), f32),
            jax.ShapeDtypeStruct((CH, 135), f32),
            jax.ShapeDtypeStruct((135, CH), f32),
        ),
        in_specs=[smem, smem, smem, vmem, vmem, vmem, vmem, vmem, anywhere],
        out_specs=(anywhere, vmem, vmem),
        scratch_shapes=[
            pltpu.VMEM((1024, 256), bf16),
            pltpu.VMEM((F, CX + 2, CY, CZ), f32),
            pltpu.VMEM((F, CX, CY, CZ), f32),
            pltpu.VMEM((F, CX, CZ), f32),
            pltpu.VMEM((F, CX, CZ), f32),
            pltpu.VMEM((2, F, CX, CZ), f32),
            pltpu.VMEM((16, CELLS), bf16),
            pltpu.VMEM((F, 18, 16, 128), f32),
            pltpu.VMEM((F, 16, 128), f32),
            pltpu.VMEM((F, 16, 128), f32),
            pltpu.VMEM((KROWS, WIDE), bf16),
            pltpu.VMEM((3 * CH, WIDE), bf16),
            pltpu.VMEM((CH, CELLS), f32),
            pltpu.VMEM((KROWS, WIDE), bf16),
            pltpu.VMEM((CH, CELLS), bf16),
            pltpu.VMEM((CH, KROWS), bf16),
            pltpu.VMEM((CH, KROWS), bf16),
            pltpu.VMEM((80, 3 * CH), bf16),
            pltpu.VMEM((TILES * 8, 128), f32),
            pltpu.VMEM((TILES * 8, 128), f32),
            pltpu.VMEM((TILES * 8, 128), f32),
            pltpu.VMEM((OWNERS * 8, 128), f32),
            pltpu.VMEM((OWNERS * 8, 128), f32),
            pltpu.VMEM((8, OWNERS, 128), f32),
            pltpu.VMEM((TILES * 8, 128), f32),
            dma,
            dma((4,)),
            dma((4,)),
            dma((INNER,)),
            dma,
            dma,
            dma,
            dma,
            dma,
            dma,
        ],
        compiler_params=pltpu.CompilerParams(vmem_limit_bytes=48 * 2**20, has_side_effects=True),
    )(
        sample_block, sample_trainer, closure_out, closure_in, closure_bias.reshape(1, CH),
        sample_trainer.reshape(1, OWNERS), first_in, last_in, brick,
    )


def on_device(
    fields, closure_in, closure_bias, closure_out, master, momentum, sample_block, sample_trainer
):
    column = lax.axis_index("gx") * lax.axis_size("gy") + lax.axis_index("gy")
    me = lax.axis_index("grp") * TRAINERS + column
    new_fields, first, last = step_call(
        sample_block,
        sample_trainer,
        closure_out,
        closure_in,
        closure_bias,
        master[:FIRST].reshape(CH, 135),
        master[FIRST:].reshape(135, CH),
        fields[0],
    )
    scaled = jnp.concatenate([first.reshape(FIRST), last.reshape(FIRST)])
    size = NPARAM // (OWNERS + TRAINERS)
    share = [lax.dynamic_slice_in_dim(whole_array, me * size, size) for whole_array in (momentum, master, scaled)]
    new_momentum = momentum_decay * share[0] + share[2]
    new_master = share[1] - outer_rate * new_momentum
    return (new_fields[None], new_master, new_momentum)


def solution(mesh):
    in_specs = (P("grp", None, "gx", "gy", None), P(), P(), P(), P(), P(), P(), P())
    out_specs = (P("grp", None, "gx", "gy", None), P(("grp", "gx", "gy")), P(("grp", "gx", "gy")))
    return jax.shard_map(
        on_device, mesh=mesh, in_specs=in_specs, out_specs=out_specs, check_vma=False
    )
```

```python
import jax
import jax.numpy as jnp
from jax import lax
from jax.experimental import pallas as pl
from jax.experimental.pallas import tpu as pltpu
from jax.sharding import PartitionSpec as P

F = 5
CH = 64
SUB = 16
CX = 16
CY = 32
CZ = 384
INNER = 3
CELLS = 4096
NPARAM = 17280
FIRST = CH * 27 * F
OWNERS = 96
TRAINERS = 32
TILES = 32
KROWS = 240
BASE = 256
WIDE = CELLS + 2 * BASE
CHUNK = 512

time_step = 0.1
base_viscosity = 0.02
viscosity_gain = 0.2
buoyancy = 0.5
inner_rate = 0.02
outer_rate = 0.01
momentum_decay = 0.9
norm_epsilon = 1e-06
f32 = jnp.float32
bf16 = jnp.bfloat16
NT = (((1,), (1,)), ((), ()))


def iota(shape, dim):
    return lax.broadcasted_iota(jnp.int32, shape, dim)


def spread_closure(closure_in, closure_bias, wide_ref):
    half = 0.5 * closure_in[...]
    inner = (((0,), (0,)), ((), ()))
    high = half.astype(bf16)
    low = (half - high.astype(f32)).astype(bf16)
    column = iota((F, 256), 1)
    fields = (iota((F, 256), 0) == column // 16 % F) & (column < 240)
    of_high = (fields & (column < 160)).astype(f32).astype(bf16)
    of_low = (fields & (column >= 160)).astype(f32).astype(bf16)
    table = lax.dot_general(high, of_high, inner, preferred_element_type=f32)
    table = table + lax.dot_general(low, of_low, inner, preferred_element_type=f32)
    diagonal = iota((CH, CH), 0) == iota((CH, CH), 1)
    bias = 0.5 * jnp.sum(jnp.where(diagonal, closure_bias[...], 0.0), axis=1, keepdims=True)
    lane = iota((CH, 256), 1)
    for place in range(240, 243):
        term = bias.astype(bf16).astype(f32)
        table = jnp.where(lane == place, term, table)
        bias = bias - term
    table = table.astype(bf16)
    for part in range(8):
        pick = (iota((128, CH), 0) // 16 + part * 8 == iota((128, CH), 1)).astype(f32).astype(bf16)
        rows = jnp.dot(pick, table, preferred_element_type=f32)
        row = iota((128, 256), 0) % 16
        column = iota((128, 256), 1)
        keep = (row == column % 16) | (column >= 240)
        wide_ref[part * 128 : (part + 1) * 128, :] = jnp.where(keep, rows, 0.0).astype(bf16)


def closure(cells, wide_ref, out_ref):
    length = cells.shape[1]
    high = cells.astype(bf16)
    low = (cells - high.astype(f32)).astype(bf16)
    stack = jnp.concatenate([high, low, high, jnp.ones((16, length), bf16)], axis=0)
    total = jnp.zeros((16, length), f32)
    for part in range(8):
        half = jnp.dot(wide_ref[part * 128 : (part + 1) * 128, :], stack, preferred_element_type=f32)
        bent = jnp.tanh(half)
        for k in range(8):
            h = half[k * 16 : (k + 1) * 16]
            t = bent[k * 16 : (k + 1) * 16]
            total = total + out_ref[part * 8 + k] * (h + h * t)
    return viscosity_gain * (jnp.maximum(total, 0.0) + jnp.log1p(jnp.exp(-jnp.abs(total))))


def advance(center, east, west, north, south, upper, lower, eddy):
    viscosity = base_viscosity + eddy
    result = []
    for f in range(F):
        laplacian = east[f] + west[f] + north[f] + south[f] + upper[f] + lower[f] - 6.0 * center[f]
        advection = (
            center[0] * (east[f] - west[f])
            + center[1] * (north[f] - south[f])
            + center[2] * (upper[f] - lower[f])
        )
        value = viscosity * laplacian - 0.5 * advection
        if f == 2:
            value = value + buoyancy * center[3]
        result.append(value)
    return result


def cut(rows, z_block):
    rolled = pltpu.roll(rows, lax.rem(CZ + 1 - z_block * 16, CZ), 1)[:, :128]
    lane = iota(rolled.shape, 1)
    outside = ((lane == 0) & (z_block == 0)) | ((lane == 17) & (z_block == 23))
    return jnp.where(outside, 0.0, rolled)


def own_windows(block, out_ref, padded, wide_ref, window, north_rows, south_rows, eddies):
    upper_half = block // 24 == 1
    z_block = block % 24
    for f in range(F):
        rows = jnp.where(upper_half, padded[f, 1 : CX + 1, 15, :], padded[f, 1 : CX + 1, 16, :])
        rows = cut(rows, z_block)
        south_rows[f] = rows
        north_rows[f] = rows

    def load(x, carry):
        for f in range(F):
            window[f, x] = cut(jnp.where(upper_half, padded[f, x, 16:, :], padded[f, x, :16, :]), z_block)
        return carry

    lax.fori_loop(1, CX + 1, load, 0, unroll=2)

    def quarter(i, carry):
        x0 = i * 4
        cells = jnp.concatenate(
            [jnp.concatenate([window[f, x0 + j + 1] for f in range(F)], axis=0) for j in range(4)], axis=1
        )
        eddies[i] = closure(cells, wide_ref, out_ref)
        return carry

    lax.fori_loop(0, 4, quarter, 0)


def cut_cube(block, y_near, payload, window, north_rows, south_rows, eddies):
    upper_half = block // 24 == 1
    for f in range(F):
        south_rows[f] = jnp.where(upper_half, south_rows[f], y_near[0, f])
        north_rows[f] = jnp.where(upper_half, y_near[1, f], north_rows[f])
    lane = iota((128, 256), 0)
    place = iota((128, 256), 1)
    unfold = (lane - 1 == place % 16).astype(f32).astype(bf16)
    own_row = iota((160, 256), 0) % 16 == iota((160, 256), 1) // 16
    group = iota((16, 160), 1) // 16
    gather = (jnp.where(group < 5, group, group + 3) == iota((16, 160), 0)).astype(f32).astype(bf16)
    row = iota((16, 128), 0)

    def quarter(i, carry):
        eddy = eddies[i]
        for j in range(4):
            x = i * 4 + j
            center = [window[f, x + 1] for f in range(F)]
            east = [window[f, x + 2] for f in range(F)]
            west = [window[f, x] for f in range(F)]
            north = [
                jnp.where(row == 15, north_rows[f, pl.ds(x, 1), :], pltpu.roll(center[f], 15, 0)) for f in range(F)
            ]
            south = [
                jnp.where(row == 0, south_rows[f, pl.ds(x, 1), :], pltpu.roll(center[f], 1, 0)) for f in range(F)
            ]
            upper = [pltpu.roll(center[f], 127, 1) for f in range(F)]
            lower = [pltpu.roll(center[f], 1, 1) for f in range(F)]
            tendency = advance(
                center, east, west, north, south, upper, lower, eddy[:, j * 128 : (j + 1) * 128]
            )
            both = jnp.concatenate(center + tendency, axis=0).astype(bf16)
            flat = jnp.dot(both, unfold, preferred_element_type=f32)
            flat = jnp.where(own_row, flat, 0.0).astype(bf16)
            flat = jnp.dot(gather, flat, preferred_element_type=f32).astype(bf16)
            payload[:, pl.ds(pl.multiple_of(x * 256, 256), 256)] = flat
        return carry

    lax.fori_loop(0, 4, quarter, 0)


def evolve(begin, end, out_ref, padded, y_low, y_high, new_fields, wide_ref):
    row = iota((CY, CZ), 0)
    lane = iota((CY, CZ), 1)

    def plane(x, carry):
        center = [padded[f, x + 1] for f in range(F)]
        cells = jnp.concatenate(
            [jnp.concatenate([c[h * 16 : (h + 1) * 16] for c in center], axis=0) for h in range(2)], axis=1
        )
        eddy = closure(cells, wide_ref, out_ref)
        eddy = jnp.concatenate([eddy[:, :CZ], eddy[:, CZ:]], axis=0)
        center = [padded[f, x + 1] for f in range(F)]
        east = [padded[f, x + 2] for f in range(F)]
        west = [padded[f, x] for f in range(F)]
        north = [
            jnp.where(row == CY - 1, y_high[f, pl.ds(x, 1), :], pltpu.roll(center[f], CY - 1, 0)) for f in range(F)
        ]
        south = [jnp.where(row == 0, y_low[f, pl.ds(x, 1), :], pltpu.roll(center[f], 1, 0)) for f in range(F)]
        upper = [jnp.where(lane == CZ - 1, 0.0, pltpu.roll(center[f], CZ - 1, 1)) for f in range(F)]
        lower = [jnp.where(lane == 0, 0.0, pltpu.roll(center[f], 1, 1)) for f in range(F)]
        tendency = advance(center, east, west, north, south, upper, lower, eddy)
        for f in range(F):
            new_fields[f, x] = center[f] + time_step * tendency[f]
        return carry

    lax.fori_loop(begin, end, plane, 0)


def shifted(values, y_step, z_step):
    length = values.shape[1]
    offset = 16 * y_step + z_step
    place = iota(values.shape, 1)
    if y_step:
        y = place // 16 % 16 + y_step
        inside = (y >= 0) & (y < 16)
    else:
        z = place % 16 + z_step
        inside = (z >= 0) & (z < 16)
    return jnp.where(inside, pltpu.roll(values, -offset % length, 1), 0.0)


STEPS = (-1, 0, 1)


def nine(values, sign):
    along_z = {s: values if s == 0 else shifted(values, 0, sign * s) for s in STEPS}
    rows = []
    for y_step in STEPS:
        for z_step in STEPS:
            part = along_z[z_step]
            rows.append(part if y_step == 0 else shifted(part, sign * y_step, 0))
    rows.append(jnp.zeros_like(values))
    return jnp.concatenate(rows, axis=0)


def build_stack(payload, stack, hiddens, errors):
    for x_step in STEPS:
        if x_step:
            block = x_step + 1
            ends = (slice(BASE, 2 * BASE), slice(CELLS, CELLS + BASE))
            edge, empty = ends if x_step < 0 else ends[::-1]
            errors[block * 80 : (block + 1) * 80, empty] = jnp.zeros((80, BASE), bf16)
            hiddens[block * CH : (block + 1) * CH, edge] = jnp.zeros((CH, BASE), bf16)
            stack[block * 80 : (block + 1) * 80, edge] = jnp.zeros((80, BASE), bf16)
    for o in range(0, CELLS, CHUNK):
        rows = nine(payload[:, o : o + CHUNK].astype(f32)[:8], 1).astype(bf16)
        for x_step in STEPS:
            at = BASE + o - BASE * x_step
            stack[(x_step + 1) * 80 : (x_step + 2) * 80, at : at + CHUNK] = rows


def table_of(tiles, layer):
    return jnp.concatenate(
        [tiles[layer * 128 : layer * 128 + 64, :], tiles[layer * 128 + 64 : layer * 128 + 128, :]], axis=1
    )


def set_table(tiles, layer, table):
    tiles[layer * 128 : layer * 128 + 64, :] = table[:, :128]
    tiles[layer * 128 + 64 : layer * 128 + 128, :] = table[:, 128:]


def gradient(scale, weights, payload, stack, hiddens, slopes, errors, pres, now_first, now_last, now_out, grad):
    eye = (iota((KROWS, KROWS), 0) == iota((KROWS, KROWS), 1)).astype(f32).astype(bf16)
    now_first[...] = table_of(weights, 0)[:, :KROWS].astype(bf16)
    last = table_of(weights, 1)[:, :KROWS].astype(bf16)
    now_last[...] = last
    turned = lax.dot_general(eye, last, NT, preferred_element_type=f32)
    now_out[...] = jnp.concatenate([turned[b * 80 : (b + 1) * 80] for b in range(3)], axis=1).astype(bf16)
    for i in range(0, CELLS, CHUNK):
        o = BASE + i
        pre = jnp.dot(now_first[...], stack[:, o : o + CHUNK], preferred_element_type=f32)
        sigmoid = 0.5 + 0.5 * jnp.tanh(0.5 * pre)
        hidden = pre * sigmoid
        slopes[:, i : i + CHUNK] = sigmoid + hidden * (1.0 - sigmoid)
        hidden = hidden.astype(bf16)
        for x_step in STEPS:
            at = o - BASE * x_step
            hiddens[(x_step + 1) * CH : (x_step + 2) * CH, at : at + CHUNK] = hidden
    for i in range(0, CELLS, CHUNK):
        o = BASE + i
        parts = jnp.dot(now_out[...], hiddens[:, o : o + CHUNK], preferred_element_type=f32)
        predicted = None
        for z_step in STEPS:
            line = None
            for y_step in STEPS:
                row = ((y_step + 1) * 3 + z_step + 1) * 8
                part = parts[row : row + 8]
                part = part if y_step == 0 else shifted(part, y_step, 0)
                line = part if line is None else line + part
            line = line if z_step == 0 else shifted(line, 0, z_step)
            predicted = line if predicted is None else predicted + line
        targets = payload[:, i : i + CHUNK].astype(f32)[8:]
        error = (scale * (predicted - targets)).astype(bf16).astype(f32)
        rows = nine(error, -1).astype(bf16)
        for x_step in STEPS:
            at = o + BASE * x_step
            errors[(x_step + 1) * 80 : (x_step + 2) * 80, at : at + CHUNK] = rows
    for i in range(0, CELLS, CHUNK):
        o = BASE + i
        back = jnp.dot(now_last[...], errors[:, o : o + CHUNK], preferred_element_type=f32)
        pres[:, i : i + CHUNK] = (back * slopes[:, i : i + CHUNK]).astype(bf16)
    cells = slice(BASE, BASE + CELLS)
    spare = jnp.zeros((CH, 256 - KROWS), f32)
    first = lax.dot_general(pres[...], stack[:, cells], NT, preferred_element_type=f32)
    set_table(grad, 0, jnp.concatenate([first, spare], axis=1))
    last = lax.dot_general(hiddens[CH : 2 * CH, cells], errors[:, cells], NT, preferred_element_type=f32)
    set_table(grad, 1, jnp.concatenate([last, spare], axis=1))


def three_terms(values):
    high = values.astype(bf16)
    rest = values - high.astype(f32)
    middle = rest.astype(bf16)
    return high, middle, (rest - middle.astype(f32)).astype(bf16)


def lane_of(offset, field):
    return offset // 9 * 80 + offset % 9 * 8 + field


def parameter_of(layer):
    lane = iota((1, 256), 1)
    rest = lane % 80
    offset, field = lane // 80 * 9 + rest // 8, rest % 8
    index = offset * F + field if layer == 0 else field * 27 + offset
    return jnp.where((lane < KROWS) & (rest < 72) & (field < F), index, -1)


def one_hot(condition):
    return condition.astype(f32).astype(bf16)


def first_table(flat):
    wide = jnp.concatenate([flat[m : m + CH] for m in range(5)], axis=1)
    unit = iota((CH, 640), 0)
    for bit in range(6):
        wide = jnp.where(unit // 2**bit % 2 == 1, pltpu.roll(wide, 640 - 7 * 2**bit, 1), wide)
    pick = one_hot(iota((256, 256), 0) == parameter_of(0))
    return jnp.dot(wide[:, :256].astype(bf16), pick, preferred_element_type=f32)


def last_table(flat):
    lane = iota((256, 1), 0)
    rest = lane % 80
    row = rest % 8 * 27 + lane // 80 * 9 + rest // 8
    valid = (lane < KROWS) & (rest < 72) & (rest % 8 < F)
    source = jnp.where(valid, 67 + (row + 1) // 2, -1)
    pick = one_hot(iota((256, 135), 1) == source)
    both = jnp.dot(pick, flat.astype(bf16), preferred_element_type=f32)
    mine = jnp.where((row + 1) % 2 == 1, both[:, CH:], both[:, :CH]).astype(bf16)
    eye = one_hot(iota((CH, CH), 0) == iota((CH, CH), 1))
    return lax.dot_general(eye, mine, NT, preferred_element_type=f32)


def share_of(first, last, me):
    of_first = me < CH
    table = jnp.where(of_first, first, last)
    place = iota((135, 1), 0)
    flat = (me - CH) * 135 + place
    row = flat // CH
    lane = jnp.where(of_first, lane_of(place // F, place % F), lane_of(row % 27, row // 27))
    pick = one_hot(iota((135, 256), 1) == lane)
    values = sum(lax.dot_general(term, pick, NT, preferred_element_type=f32) for term in three_terms(table))
    along = iota((CH, 135), 1)
    unit = jnp.where(of_first, me, ((me - CH) * 135 + along) % CH)
    return jnp.sum(jnp.where(iota((CH, 135), 0) == unit, values, 0.0), axis=0, keepdims=True)


def device(group, column):
    columns = lax.axis_size("gy")
    return {"grp": group, "gx": column // columns, "gy": lax.rem(column, columns)}


def whole(ref, sem):
    return pltpu.make_async_copy(ref, ref, sem)


def step_kernel(
    block_in, trainer_in, out_in, closure_in_, closure_bias_, trainer_row_, flat_in_, brick,
    new_fields, share,
    block_ref, trainer_ref, out_ref, closure_in, closure_bias, trainer_row, flat_in,
    wide_ref, padded, y_low, y_high, y_send, payload, window, north_rows, south_rows, eddies, x_near_send, y_near_send, y_near,
    stack, hiddens, slopes, errors, pres, now_first, now_last, now_out,
    start, weights, grad, gathered, answer, running, delta,
    small_sems, load_sem, near_send, near_recv, halo_send, halo_recv,
    up_send, up_recv, down_send, down_recv, last_send, last_recv,
):
    group = lax.axis_index("grp")
    column = lax.axis_index("gx") * lax.axis_size("gy") + lax.axis_index("gy")
    me = group * TRAINERS + column
    last_group = lax.axis_size("grp") - 1
    sources = (block_in, trainer_in, out_in, closure_in_, closure_bias_, trainer_row_, flat_in_)
    places_in = (block_ref, trainer_ref, out_ref, closure_in, closure_bias, trainer_row, flat_in)
    small = [
        pltpu.make_async_copy(source, to, small_sems.at[i]) for i, (source, to) in enumerate(zip(sources, places_in))
    ]
    for copy in small:
        copy.start()

    def start_tables():
        flat = flat_in[...]
        set_table(start, 0, first_table(flat))
        set_table(start, 1, last_table(flat))

    @pl.when(group < last_group)
    def _():
        load = pltpu.make_async_copy(brick, padded.at[:, pl.ds(1, CX)], load_sem)
        load.start()
        for copy in small:
            copy.wait()
        gx, gy = lax.axis_index("gx"), lax.axis_index("gy")
        gx_size, gy_size = lax.axis_size("gx"), lax.axis_size("gy")
        x_next, x_last = lax.rem(gx + 1, gx_size), lax.rem(gx + gx_size - 1, gx_size)
        y_next, y_last = lax.rem(gy + 1, gy_size), lax.rem(gy + gy_size - 1, gy_size)
        first_owner = group * TRAINERS
        load.wait()
        near = []
        for side, to in enumerate((x_next, x_last)):
            block = block_ref[first_owner + to * gy_size + gy]
            plane = CX if side == 0 else 1
            for f in range(F):
                rows = jnp.where(block // 24 == 1, padded[f, plane, 16:, :], padded[f, plane, :16, :])
                x_near_send[side, f] = cut(rows, block % 24)
            copy = pltpu.make_async_remote_copy(
                x_near_send.at[side],
                window.at[:, 0 if side == 0 else CX + 1],
                near_send.at[side],
                near_recv.at[side],
                device_id={"gx": to},
            )
            copy.start()
            near.append(copy)
        for side, to in enumerate((y_next, y_last)):
            block = block_ref[first_owner + gx * gy_size + to]
            line = CY - 1 if side == 0 else 0
            for f in range(F):
                rows = padded[f, 1 : CX + 1, line, :]
                y_send[side, f] = rows
                y_near_send[side, f] = cut(rows, block % 24)
            copy = pltpu.make_async_remote_copy(
                y_near_send.at[side],
                y_near.at[side],
                near_send.at[2 + side],
                near_recv.at[2 + side],
                device_id={"gy": to},
            )
            copy.start()
            near.append(copy)
        spread_closure(closure_in, closure_bias, wide_ref)
        own_block = block_ref[me]
        own_windows(own_block, out_ref, padded, wide_ref, window, north_rows, south_rows, eddies)
        start_tables()
        same = (trainer_row[...] == trainer_ref[me]).astype(f32)
        count = jnp.sum(same, axis=1, keepdims=True)
        scale = 2.0 * (1.0 / (count * CELLS))
        for copy in near:
            copy.wait()
        halos = [
            pltpu.make_async_remote_copy(
                brick.at[:, CX - 1], padded.at[:, 0], halo_send.at[0], halo_recv.at[0], device_id={"gx": x_next}
            ),
            pltpu.make_async_remote_copy(
                brick.at[:, 0], padded.at[:, CX + 1], halo_send.at[1], halo_recv.at[1], device_id={"gx": x_last}
            ),
            pltpu.make_async_remote_copy(
                y_send.at[0], y_low, halo_send.at[2], halo_recv.at[2], device_id={"gy": y_next}
            ),
            pltpu.make_async_remote_copy(
                y_send.at[1], y_high, halo_send.at[3], halo_recv.at[3], device_id={"gy": y_last}
            ),
        ]
        for copy in halos:
            copy.start()
        cut_cube(own_block, y_near, payload, window, north_rows, south_rows, eddies)
        build_stack(payload, stack, hiddens, errors)
        bounds = (0, 5, 10, CX)
        for k in range(INNER):
            gradient(
                scale, weights if k else start, payload, stack, hiddens, slopes, errors, pres,
                now_first, now_last, now_out, grad,
            )

            def send(j, carry):
                to = lax.rem(column + j, TILES)
                pltpu.make_async_remote_copy(
                    grad.at[pl.ds(pl.multiple_of(to * 8, 8), 8)],
                    gathered.at[pl.ds(pl.multiple_of(me * 8, 8), 8)],
                    up_send,
                    up_recv,
                    device_id=device(last_group, to),
                ).start()
                return carry

            lax.fori_loop(0, TILES, send, 0, unroll=4)
            if k == 0:
                for copy in halos:
                    copy.wait()
            evolve(bounds[k], bounds[k + 1], out_ref, padded, y_low, y_high, new_fields, wide_ref)
            whole(grad, up_send).wait()
            if k < INNER - 1:
                whole(weights, down_recv).wait()
        whole(delta, last_recv).wait()

    @pl.when(group == last_group)
    def _():
        keep = pltpu.make_async_copy(brick, new_fields, load_sem)
        keep.start()
        for copy in small:
            copy.wait()
        start_tables()
        own_start = start[pl.ds(pl.multiple_of(column * 8, 8), 8), :]
        square = (OWNERS, OWNERS)
        across = jnp.broadcast_to(trainer_row[...].astype(f32), square)
        diagonal = jnp.where(iota(square, 0) == iota(square, 1), across, 0.0)
        down = jnp.sum(diagonal, axis=1, keepdims=True)
        same = (across == down).astype(f32).astype(bf16)
        running[...] = jnp.zeros_like(running)
        total = jnp.zeros((8, 128), f32)
        for k in range(INNER):
            whole(gathered, up_recv).wait()

            def add(o, total):
                return total + gathered[pl.ds(pl.multiple_of(o * 8, 8), 8), :]

            total = lax.fori_loop(0, OWNERS, add, total, unroll=8)
            if k < INNER - 1:
                if k:
                    whole(answer, down_send).wait()
                for r in range(8):
                    terms = three_terms(gathered[pl.ds(r, OWNERS, stride=8), :])
                    part = sum(jnp.dot(same, term, preferred_element_type=f32) for term in terms)
                    part = running[r] + part
                    running[r] = part
                    answer[pl.ds(r, OWNERS, stride=8), :] = own_start[r : r + 1] - inner_rate * part

                def send(j, carry):
                    to = lax.rem(column + j, TRAINERS)
                    for g in range(OWNERS // TRAINERS):
                        pltpu.make_async_remote_copy(
                            answer.at[pl.ds(pl.multiple_of((g * TRAINERS + to) * 8, 8), 8)],
                            weights.at[pl.ds(pl.multiple_of(column * 8, 8), 8)],
                            down_send,
                            down_recv,
                            device_id=device(g, to),
                        ).start()
                    return carry

                lax.fori_loop(0, TRAINERS, send, 0, unroll=2)
        whole(answer, down_send).wait()
        own = delta.at[pl.ds(pl.multiple_of(column * 8, 8), 8)]
        own[...] = inner_rate * total

        def tell(j, carry):
            to = lax.rem(me + j, OWNERS + TRAINERS)
            pltpu.make_async_remote_copy(
                own, own, last_send, last_recv, device_id=device(to // TRAINERS, lax.rem(to, TRAINERS))
            ).start()
            return carry

        lax.fori_loop(1, OWNERS + TRAINERS, tell, 0)
        others = delta.at[pl.ds(0, (TILES - 1) * 8)]
        whole(others, last_recv).wait()
        for part in range(3):
            whole(delta, last_send).wait()
        whole(others, last_send).wait()
        keep.wait()

    values = delta[...]
    inverse = lax.rsqrt(jnp.sum(values * values) / NPARAM + norm_epsilon)
    share[...] = inverse * share_of(table_of(delta, 0), table_of(delta, 1), me)


def step_call(sample_block, sample_trainer, closure_out, closure_in, closure_bias, master, brick):
    vmem = pl.BlockSpec(memory_space=pltpu.VMEM)
    hbm = pl.BlockSpec(memory_space=pltpu.HBM)
    dma = pltpu.SemaphoreType.DMA
    operands = (
        sample_block, sample_trainer, closure_out, closure_in.T, closure_bias.reshape(1, CH),
        sample_trainer.reshape(1, OWNERS), master.reshape(135, 128), brick,
    )
    spaces = [pltpu.SMEM] * 3 + [pltpu.VMEM] * 4
    return pl.pallas_call(
        step_kernel,
        out_shape=(
            jax.ShapeDtypeStruct((F, CX, CY, CZ), f32),
            jax.ShapeDtypeStruct((1, 135), f32),
        ),
        in_specs=[hbm] * 8,
        out_specs=(vmem, vmem),
        scratch_shapes=[space(x.shape, x.dtype) for space, x in zip(spaces, operands)]
        + [
            pltpu.VMEM((1024, 256), bf16),
            pltpu.VMEM((F, CX + 2, CY, CZ), f32),
            pltpu.VMEM((F, CX, CZ), f32),
            pltpu.VMEM((F, CX, CZ), f32),
            pltpu.VMEM((2, F, CX, CZ), f32),
            pltpu.VMEM((16, CELLS), bf16),
            pltpu.VMEM((F, 18, 16, 128), f32),
            pltpu.VMEM((F, 16, 128), f32),
            pltpu.VMEM((F, 16, 128), f32),
            pltpu.VMEM((4, 16, 512), f32),
            pltpu.VMEM((2, F, 16, 128), f32),
            pltpu.VMEM((2, F, 16, 128), f32),
            pltpu.VMEM((2, F, 16, 128), f32),
            pltpu.VMEM((KROWS, WIDE), bf16),
            pltpu.VMEM((3 * CH, WIDE), bf16),
            pltpu.VMEM((CH, CELLS), f32),
            pltpu.VMEM((KROWS, WIDE), bf16),
            pltpu.VMEM((CH, CELLS), bf16),
            pltpu.VMEM((CH, KROWS), bf16),
            pltpu.VMEM((CH, KROWS), bf16),
            pltpu.VMEM((80, 3 * CH), bf16),
            pltpu.VMEM((TILES * 8, 128), f32),
            pltpu.VMEM((TILES * 8, 128), f32),
            pltpu.VMEM((TILES * 8, 128), f32),
            pltpu.VMEM((OWNERS * 8, 128), f32),
            pltpu.VMEM((OWNERS * 8, 128), f32),
            pltpu.VMEM((8, OWNERS, 128), f32),
            pltpu.VMEM((TILES * 8, 128), f32),
            dma((7,)),
            dma,
            dma((4,)),
            dma((4,)),
            dma((4,)),
            dma((4,)),
            dma,
            dma,
            dma,
            dma,
            dma,
            dma,
        ],
        compiler_params=pltpu.CompilerParams(vmem_limit_bytes=60 * 2**20, has_side_effects=True),
    )(*operands)


def finish_kernel(made, share, momentum, master, new_fields, new_master, new_momentum, held, in_sems, out_sems):
    into = [pltpu.make_async_copy(made.at[f], held.at[f], in_sems.at[f]) for f in range(F)]
    out = [pltpu.make_async_copy(held.at[f], new_fields.at[f], out_sems.at[f]) for f in range(F)]
    for copy in into:
        copy.start()
    columns = lax.axis_size("gy")
    me = lax.axis_index("grp") * TRAINERS + lax.axis_index("gx") * columns + lax.axis_index("gy")
    begin = me * 135
    row = begin // 128

    def mine(flat):
        rows = [flat[pl.ds(jnp.minimum(row + i, 134), 1), :] for i in range(3)]
        wide = jnp.broadcast_to(jnp.concatenate(rows, axis=1), (8, 384))
        return pltpu.roll(wide, lax.rem(384 - begin % 128, 384), 1)[:1, :135]

    momentum_share = momentum_decay * mine(momentum) + share[...]
    new_momentum[...] = momentum_share
    new_master[...] = mine(master) - outer_rate * momentum_share
    for f in range(F):
        into[f].wait()
        out[f].start()
    for f in range(F):
        out[f].wait()


def finish_call(made, share, momentum, master):
    vmem = pl.BlockSpec(memory_space=pltpu.VMEM)
    hbm = pl.BlockSpec(memory_space=pltpu.HBM)
    part = jax.ShapeDtypeStruct((1, 135), f32)
    return pl.pallas_call(
        finish_kernel,
        out_shape=(jax.ShapeDtypeStruct(made.shape, made.dtype), part, part),
        in_specs=[hbm, vmem, vmem, vmem],
        out_specs=(hbm, vmem, vmem),
        scratch_shapes=[
            pltpu.VMEM(made.shape, f32),
            pltpu.SemaphoreType.DMA((F,)),
            pltpu.SemaphoreType.DMA((F,)),
        ],
        compiler_params=pltpu.CompilerParams(vmem_limit_bytes=60 * 2**20),
    )(made, share, momentum.reshape(135, 128), master.reshape(135, 128))


def on_device(
    fields, closure_in, closure_bias, closure_out, master, momentum, sample_block, sample_trainer
):
    made, share = step_call(
        sample_block, sample_trainer, closure_out, closure_in, closure_bias, master, fields[0]
    )
    new_fields, new_master, new_momentum = finish_call(made, share, momentum, master)
    return (new_fields[None], new_master.reshape(135), new_momentum.reshape(135))


def solution(mesh):
    in_specs = (P("grp", None, "gx", "gy", None), P(), P(), P(), P(), P(), P(), P())
    out_specs = (P("grp", None, "gx", "gy", None), P(("grp", "gx", "gy")), P(("grp", "gx", "gy")))
    return jax.shard_map(
        on_device, mesh=mesh, in_specs=in_specs, out_specs=out_specs, check_vma=False
    )
```

```python
import jax
import jax.numpy as jnp
from jax import lax
from jax.experimental import pallas as pl
from jax.experimental.pallas import tpu as pltpu
from jax.sharding import PartitionSpec as P

F = 5
CH = 64
SUB = 16
CX = 16
CY = 32
CZ = 384
INNER = 3
CELLS = 4096
NPARAM = 17280
FIRST = CH * 27 * F
OWNERS = 96
TRAINERS = 32
TILES = 32
KROWS = 240
BASE = 256
WIDE = CELLS + 2 * BASE
CHUNK = 512

time_step = 0.1
base_viscosity = 0.02
viscosity_gain = 0.2
buoyancy = 0.5
inner_rate = 0.02
outer_rate = 0.01
momentum_decay = 0.9
norm_epsilon = 1e-06
f32 = jnp.float32
MESH = pl.DeviceIdType.MESH
bf16 = jnp.bfloat16
NT = (((1,), (1,)), ((), ()))


def iota(shape, dim):
    return lax.broadcasted_iota(jnp.int32, shape, dim)


def spread_closure(closure_in, closure_bias, wide_ref):
    half = 0.5 * closure_in[...]
    inner = (((0,), (0,)), ((), ()))
    high = half.astype(bf16)
    low = (half - high.astype(f32)).astype(bf16)
    column = iota((F, 256), 1)
    fields = (iota((F, 256), 0) == column // 16 % F) & (column < 240)
    of_high = (fields & (column < 160)).astype(f32).astype(bf16)
    of_low = (fields & (column >= 160)).astype(f32).astype(bf16)
    table = lax.dot_general(high, of_high, inner, preferred_element_type=f32)
    table = table + lax.dot_general(low, of_low, inner, preferred_element_type=f32)
    diagonal = iota((CH, CH), 0) == iota((CH, CH), 1)
    bias = 0.5 * jnp.sum(jnp.where(diagonal, closure_bias[...], 0.0), axis=1, keepdims=True)
    lane = iota((CH, 256), 1)
    for place in range(240, 243):
        term = bias.astype(bf16).astype(f32)
        table = jnp.where(lane == place, term, table)
        bias = bias - term
    table = table.astype(bf16)
    for part in range(8):
        pick = (iota((128, CH), 0) // 16 + part * 8 == iota((128, CH), 1)).astype(f32).astype(bf16)
        rows = jnp.dot(pick, table, preferred_element_type=f32)
        row = iota((128, 256), 0) % 16
        column = iota((128, 256), 1)
        keep = (row == column % 16) | (column >= 240)
        wide_ref[part * 128 : (part + 1) * 128, :] = jnp.where(keep, rows, 0.0).astype(bf16)


def closure(cells, wide_ref, out_ref):
    length = cells.shape[1]
    high = cells.astype(bf16)
    low = (cells - high.astype(f32)).astype(bf16)
    stack = jnp.concatenate([high, low, high, jnp.ones((16, length), bf16)], axis=0)
    total = jnp.zeros((16, length), f32)
    for part in range(8):
        half = jnp.dot(wide_ref[part * 128 : (part + 1) * 128, :], stack, preferred_element_type=f32)
        bent = jnp.tanh(half)
        for k in range(8):
            h = half[k * 16 : (k + 1) * 16]
            t = bent[k * 16 : (k + 1) * 16]
            total = total + out_ref[part * 8 + k] * (h + h * t)
    return viscosity_gain * (jnp.maximum(total, 0.0) + jnp.log1p(jnp.exp(-jnp.abs(total))))


def advance(center, east, west, north, south, upper, lower, eddy):
    viscosity = base_viscosity + eddy
    result = []
    for f in range(F):
        laplacian = east[f] + west[f] + north[f] + south[f] + upper[f] + lower[f] - 6.0 * center[f]
        advection = (
            center[0] * (east[f] - west[f])
            + center[1] * (north[f] - south[f])
            + center[2] * (upper[f] - lower[f])
        )
        value = viscosity * laplacian - 0.5 * advection
        if f == 2:
            value = value + buoyancy * center[3]
        result.append(value)
    return result


def cut(rows, z_block):
    rolled = pltpu.roll(rows, lax.rem(CZ + 1 - z_block * 16, CZ), 1)[:, :128]
    lane = iota(rolled.shape, 1)
    outside = ((lane == 0) & (z_block == 0)) | ((lane == 17) & (z_block == 23))
    return jnp.where(outside, 0.0, rolled)


def own_windows(block, out_ref, padded, wide_ref, window, north_rows, south_rows, eddies):
    upper_half = block // 24 == 1
    z_block = block % 24
    for f in range(F):
        rows = jnp.where(upper_half, padded[f, 1 : CX + 1, 15, :], padded[f, 1 : CX + 1, 16, :])
        rows = cut(rows, z_block)
        south_rows[f] = rows
        north_rows[f] = rows

    def load(x, carry):
        for f in range(F):
            window[f, x] = cut(jnp.where(upper_half, padded[f, x, 16:, :], padded[f, x, :16, :]), z_block)
        return carry

    lax.fori_loop(1, CX + 1, load, 0, unroll=2)

    def quarter(i, carry):
        x0 = i * 4
        cells = jnp.concatenate(
            [jnp.concatenate([window[f, x0 + j + 1] for f in range(F)], axis=0) for j in range(4)], axis=1
        )
        eddies[i] = closure(cells, wide_ref, out_ref)
        return carry

    lax.fori_loop(0, 4, quarter, 0)


def cut_cube(block, y_near, payload, window, north_rows, south_rows, eddies):
    upper_half = block // 24 == 1
    for f in range(F):
        south_rows[f] = jnp.where(upper_half, south_rows[f], y_near[0, f])
        north_rows[f] = jnp.where(upper_half, y_near[1, f], north_rows[f])
    lane = iota((128, 256), 0)
    place = iota((128, 256), 1)
    unfold = (lane - 1 == place % 16).astype(f32).astype(bf16)
    own_row = iota((160, 256), 0) % 16 == iota((160, 256), 1) // 16
    group = iota((16, 160), 1) // 16
    gather = (jnp.where(group < 5, group, group + 3) == iota((16, 160), 0)).astype(f32).astype(bf16)
    row = iota((16, 128), 0)

    def quarter(i, carry):
        eddy = eddies[i]
        for j in range(4):
            x = i * 4 + j
            center = [window[f, x + 1] for f in range(F)]
            east = [window[f, x + 2] for f in range(F)]
            west = [window[f, x] for f in range(F)]
            north = [
                jnp.where(row == 15, north_rows[f, pl.ds(x, 1), :], pltpu.roll(center[f], 15, 0)) for f in range(F)
            ]
            south = [
                jnp.where(row == 0, south_rows[f, pl.ds(x, 1), :], pltpu.roll(center[f], 1, 0)) for f in range(F)
            ]
            upper = [pltpu.roll(center[f], 127, 1) for f in range(F)]
            lower = [pltpu.roll(center[f], 1, 1) for f in range(F)]
            tendency = advance(
                center, east, west, north, south, upper, lower, eddy[:, j * 128 : (j + 1) * 128]
            )
            both = jnp.concatenate(center + tendency, axis=0).astype(bf16)
            flat = jnp.dot(both, unfold, preferred_element_type=f32)
            flat = jnp.where(own_row, flat, 0.0).astype(bf16)
            flat = jnp.dot(gather, flat, preferred_element_type=f32).astype(bf16)
            payload[:, pl.ds(pl.multiple_of(x * 256, 256), 256)] = flat
        return carry

    lax.fori_loop(0, 4, quarter, 0)


def evolve(begin, end, out_ref, padded, y_low, y_high, new_fields, wide_ref):
    row = iota((CY, CZ), 0)
    lane = iota((CY, CZ), 1)

    def plane(x, carry):
        center = [padded[f, x + 1] for f in range(F)]
        cells = jnp.concatenate(
            [jnp.concatenate([c[h * 16 : (h + 1) * 16] for c in center], axis=0) for h in range(2)], axis=1
        )
        eddy = closure(cells, wide_ref, out_ref)
        eddy = jnp.concatenate([eddy[:, :CZ], eddy[:, CZ:]], axis=0)
        center = [padded[f, x + 1] for f in range(F)]
        east = [padded[f, x + 2] for f in range(F)]
        west = [padded[f, x] for f in range(F)]
        north = [
            jnp.where(row == CY - 1, y_high[f, pl.ds(x, 1), :], pltpu.roll(center[f], CY - 1, 0)) for f in range(F)
        ]
        south = [jnp.where(row == 0, y_low[f, pl.ds(x, 1), :], pltpu.roll(center[f], 1, 0)) for f in range(F)]
        upper = [jnp.where(lane == CZ - 1, 0.0, pltpu.roll(center[f], CZ - 1, 1)) for f in range(F)]
        lower = [jnp.where(lane == 0, 0.0, pltpu.roll(center[f], 1, 1)) for f in range(F)]
        tendency = advance(center, east, west, north, south, upper, lower, eddy)
        for f in range(F):
            new_fields[f, x] = center[f] + time_step * tendency[f]
        return carry

    lax.fori_loop(begin, end, plane, 0)


def shifted(values, y_step, z_step):
    length = values.shape[1]
    offset = 16 * y_step + z_step
    place = iota(values.shape, 1)
    if y_step:
        y = place // 16 % 16 + y_step
        inside = (y >= 0) & (y < 16)
    else:
        z = place % 16 + z_step
        inside = (z >= 0) & (z < 16)
    return jnp.where(inside, pltpu.roll(values, -offset % length, 1), 0.0)


STEPS = (-1, 0, 1)


def nine(values, sign):
    along_z = {s: values if s == 0 else shifted(values, 0, sign * s) for s in STEPS}
    rows = []
    for y_step in STEPS:
        for z_step in STEPS:
            part = along_z[z_step]
            rows.append(part if y_step == 0 else shifted(part, sign * y_step, 0))
    rows.append(jnp.zeros_like(values))
    return jnp.concatenate(rows, axis=0)


def build_stack(payload, stack, hiddens, errors):
    for x_step in STEPS:
        if x_step:
            block = x_step + 1
            ends = (slice(BASE, 2 * BASE), slice(CELLS, CELLS + BASE))
            edge, empty = ends if x_step < 0 else ends[::-1]
            errors[block * 80 : (block + 1) * 80, empty] = jnp.zeros((80, BASE), bf16)
            hiddens[block * CH : (block + 1) * CH, edge] = jnp.zeros((CH, BASE), bf16)
            stack[block * 80 : (block + 1) * 80, edge] = jnp.zeros((80, BASE), bf16)
    for o in range(0, CELLS, CHUNK):
        rows = nine(payload[:, o : o + CHUNK].astype(f32)[:8], 1).astype(bf16)
        for x_step in STEPS:
            at = BASE + o - BASE * x_step
            stack[(x_step + 1) * 80 : (x_step + 2) * 80, at : at + CHUNK] = rows


def table_of(tiles, layer):
    return jnp.concatenate(
        [tiles[layer * 128 : layer * 128 + 64, :], tiles[layer * 128 + 64 : layer * 128 + 128, :]], axis=1
    )


def set_table(tiles, layer, table):
    tiles[layer * 128 : layer * 128 + 64, :] = table[:, :128]
    tiles[layer * 128 + 64 : layer * 128 + 128, :] = table[:, 128:]


def gradient(scale, weights, payload, stack, hiddens, slopes, errors, pres, now_first, now_last, now_out, grad):
    eye = (iota((KROWS, KROWS), 0) == iota((KROWS, KROWS), 1)).astype(f32).astype(bf16)
    now_first[...] = table_of(weights, 0)[:, :KROWS].astype(bf16)
    last = table_of(weights, 1)[:, :KROWS].astype(bf16)
    now_last[...] = last
    turned = lax.dot_general(eye, last, NT, preferred_element_type=f32)
    now_out[...] = jnp.concatenate([turned[b * 80 : (b + 1) * 80] for b in range(3)], axis=1).astype(bf16)
    for i in range(0, CELLS, CHUNK):
        o = BASE + i
        pre = jnp.dot(now_first[...], stack[:, o : o + CHUNK], preferred_element_type=f32)
        sigmoid = 0.5 + 0.5 * jnp.tanh(0.5 * pre)
        hidden = pre * sigmoid
        slopes[:, i : i + CHUNK] = sigmoid + hidden * (1.0 - sigmoid)
        hidden = hidden.astype(bf16)
        for x_step in STEPS:
            at = o - BASE * x_step
            hiddens[(x_step + 1) * CH : (x_step + 2) * CH, at : at + CHUNK] = hidden
    for i in range(0, CELLS, CHUNK):
        o = BASE + i
        parts = jnp.dot(now_out[...], hiddens[:, o : o + CHUNK], preferred_element_type=f32)
        predicted = None
        for z_step in STEPS:
            line = None
            for y_step in STEPS:
                row = ((y_step + 1) * 3 + z_step + 1) * 8
                part = parts[row : row + 8]
                part = part if y_step == 0 else shifted(part, y_step, 0)
                line = part if line is None else line + part
            line = line if z_step == 0 else shifted(line, 0, z_step)
            predicted = line if predicted is None else predicted + line
        targets = payload[:, i : i + CHUNK].astype(f32)[8:]
        error = (scale * (predicted - targets)).astype(bf16).astype(f32)
        rows = nine(error, -1).astype(bf16)
        for x_step in STEPS:
            at = o + BASE * x_step
            errors[(x_step + 1) * 80 : (x_step + 2) * 80, at : at + CHUNK] = rows
    for i in range(0, CELLS, CHUNK):
        o = BASE + i
        back = jnp.dot(now_last[...], errors[:, o : o + CHUNK], preferred_element_type=f32)
        pres[:, i : i + CHUNK] = (back * slopes[:, i : i + CHUNK]).astype(bf16)
    cells = slice(BASE, BASE + CELLS)
    spare = jnp.zeros((CH, 256 - KROWS), f32)
    first = lax.dot_general(pres[...], stack[:, cells], NT, preferred_element_type=f32)
    set_table(grad, 0, jnp.concatenate([first, spare], axis=1))
    last = lax.dot_general(hiddens[CH : 2 * CH, cells], errors[:, cells], NT, preferred_element_type=f32)
    set_table(grad, 1, jnp.concatenate([last, spare], axis=1))


def three_terms(values):
    high = values.astype(bf16)
    rest = values - high.astype(f32)
    middle = rest.astype(bf16)
    return high, middle, (rest - middle.astype(f32)).astype(bf16)


def lane_of(offset, field):
    return offset // 9 * 80 + offset % 9 * 8 + field


def parameter_of(layer):
    lane = iota((1, 256), 1)
    rest = lane % 80
    offset, field = lane // 80 * 9 + rest // 8, rest % 8
    index = offset * F + field if layer == 0 else field * 27 + offset
    return jnp.where((lane < KROWS) & (rest < 72) & (field < F), index, -1)


def one_hot(condition):
    return condition.astype(f32).astype(bf16)


def first_table(flat):
    wide = jnp.concatenate([flat[m : m + CH] for m in range(5)], axis=1)
    unit = iota((CH, 640), 0)
    for bit in range(6):
        wide = jnp.where(unit // 2**bit % 2 == 1, pltpu.roll(wide, 640 - 7 * 2**bit, 1), wide)
    pick = one_hot(iota((256, 256), 0) == parameter_of(0))
    return jnp.dot(wide[:, :256].astype(bf16), pick, preferred_element_type=f32)


def last_table(flat):
    lane = iota((256, 1), 0)
    rest = lane % 80
    row = rest % 8 * 27 + lane // 80 * 9 + rest // 8
    valid = (lane < KROWS) & (rest < 72) & (rest % 8 < F)
    source = jnp.where(valid, 67 + (row + 1) // 2, -1)
    pick = one_hot(iota((256, 135), 1) == source)
    both = jnp.dot(pick, flat.astype(bf16), preferred_element_type=f32)
    mine = jnp.where((row + 1) % 2 == 1, both[:, CH:], both[:, :CH]).astype(bf16)
    eye = one_hot(iota((CH, CH), 0) == iota((CH, CH), 1))
    return lax.dot_general(eye, mine, NT, preferred_element_type=f32)


def share_of(first, last, me):
    of_first = me < CH
    table = jnp.where(of_first, first, last)
    place = iota((135, 1), 0)
    flat = (me - CH) * 135 + place
    row = flat // CH
    lane = jnp.where(of_first, lane_of(place // F, place % F), lane_of(row % 27, row // 27))
    pick = one_hot(iota((135, 256), 1) == lane)
    values = sum(lax.dot_general(term, pick, NT, preferred_element_type=f32) for term in three_terms(table))
    along = iota((CH, 135), 1)
    unit = jnp.where(of_first, me, ((me - CH) * 135 + along) % CH)
    return jnp.sum(jnp.where(iota((CH, 135), 0) == unit, values, 0.0), axis=0, keepdims=True)


def device(group, column):
    columns = lax.axis_size("gy")
    return {"grp": group, "gx": column // columns, "gy": lax.rem(column, columns)}


def far_first(column, j):
    def offset(t):
        return (2 + 3 * t + 3 * (t // 2) + 2 * (t // 3)) % 4

    gx, gy = column // 4, lax.rem(column, 4)
    z = lax.rem(gx // 2 + offset(j // 8), 4)
    y = lax.rem(gx + 1 - lax.rem(j, 2), 2)
    x = lax.rem(gy + offset(lax.rem(j // 2, 4)), 4)
    return (z * 2 + y) * 4 + x


def whole(ref, sem):
    return pltpu.make_async_copy(ref, ref, sem)


def step_kernel(
    block_in, trainer_in, out_in, closure_in_, closure_bias_, trainer_row_, flat_in_, brick,
    new_fields, share,
    block_ref, trainer_ref, out_ref, closure_in, closure_bias, trainer_row, flat_in,
    wide_ref, padded, y_low, y_high, y_send, payload, window, north_rows, south_rows, eddies, x_near_send, y_near_send, y_near,
    stack, hiddens, slopes, errors, pres, now_first, now_last, now_out,
    start, weights, grad, gathered, answer, running, delta,
    small_sems, load_sem, near_send, near_recv, halo_send, halo_recv,
    up_send, up_recv, down_send, down_recv, last_send, last_recv, hand_send,
):
    group = lax.axis_index("grp")
    column = lax.axis_index("gx") * lax.axis_size("gy") + lax.axis_index("gy")
    me = group * TRAINERS + column
    last_group = lax.axis_size("grp") - 1
    barrier = pltpu.get_barrier_semaphore()
    sources = (block_in, trainer_in, out_in, closure_in_, closure_bias_, trainer_row_, flat_in_)
    places_in = (block_ref, trainer_ref, out_ref, closure_in, closure_bias, trainer_row, flat_in)
    small = [
        pltpu.make_async_copy(source, to, small_sems.at[i]) for i, (source, to) in enumerate(zip(sources, places_in))
    ]
    for copy in small:
        copy.start()

    def start_tables():
        flat = flat_in[...]
        set_table(start, 0, first_table(flat))
        set_table(start, 1, last_table(flat))

    @pl.when(group < last_group)
    def _():
        load = pltpu.make_async_copy(brick, padded.at[:, pl.ds(1, CX)], load_sem)
        load.start()
        gx, gy = lax.axis_index("gx"), lax.axis_index("gy")
        gx_size, gy_size = lax.axis_size("gx"), lax.axis_size("gy")
        x_next, x_last = lax.rem(gx + 1, gx_size), lax.rem(gx + gx_size - 1, gx_size)
        y_next, y_last = lax.rem(gy + 1, gy_size), lax.rem(gy + gy_size - 1, gy_size)

        def greet(j, carry):
            pl.semaphore_signal(barrier, 1, device_id=device(last_group, far_first(column, j)), device_id_type=MESH)
            return carry

        lax.fori_loop(0, TRAINERS, greet, 0)
        for to in (x_next, x_last):
            pl.semaphore_signal(barrier, 1, device_id={"gx": to}, device_id_type=MESH)
        for to in (y_next, y_last):
            pl.semaphore_signal(barrier, 1, device_id={"gy": to}, device_id_type=MESH)

        before = lax.rem(group + last_group - 1, last_group)
        pl.semaphore_signal(barrier, 1, device_id={"grp": before}, device_id_type=MESH)

        for copy in small:
            copy.wait()
        spread_closure(closure_in, closure_bias, wide_ref)
        first_owner = group * TRAINERS
        load.wait()
        near = []
        for side, to in enumerate((x_next, x_last)):
            block = block_ref[first_owner + to * gy_size + gy]
            plane = CX if side == 0 else 1
            for f in range(F):
                rows = jnp.where(block // 24 == 1, padded[f, plane, 16:, :], padded[f, plane, :16, :])
                x_near_send[side, f] = cut(rows, block % 24)
            near.append(
                pltpu.make_async_remote_copy(
                    x_near_send.at[side],
                    window.at[:, 0 if side == 0 else CX + 1],
                    near_send.at[side],
                    near_recv.at[side],
                    device_id={"gx": to},
                )
            )
        for side, to in enumerate((y_next, y_last)):
            block = block_ref[first_owner + gx * gy_size + to]
            line = CY - 1 if side == 0 else 0
            for f in range(F):
                rows = padded[f, 1 : CX + 1, line, :]
                y_send[side, f] = rows
                y_near_send[side, f] = cut(rows, block % 24)
            near.append(
                pltpu.make_async_remote_copy(
                    y_near_send.at[side],
                    y_near.at[side],
                    near_send.at[2 + side],
                    near_recv.at[2 + side],
                    device_id={"gy": to},
                )
            )
        own_block = block_ref[me]
        own_windows(own_block, out_ref, padded, wide_ref, window, north_rows, south_rows, eddies)
        pl.semaphore_wait(barrier, TRAINERS + 5)
        halos = [
            pltpu.make_async_remote_copy(
                brick.at[:, CX - 1], padded.at[:, 0], halo_send.at[0], halo_recv.at[0], device_id={"gx": x_next}
            ),
            pltpu.make_async_remote_copy(
                brick.at[:, 0], padded.at[:, CX + 1], halo_send.at[1], halo_recv.at[1], device_id={"gx": x_last}
            ),
            pltpu.make_async_remote_copy(
                y_send.at[0], y_low, halo_send.at[2], halo_recv.at[2], device_id={"gy": y_next}
            ),
            pltpu.make_async_remote_copy(
                y_send.at[1], y_high, halo_send.at[3], halo_recv.at[3], device_id={"gy": y_last}
            ),
        ]
        for copy in near + halos:
            copy.start()
        start_tables()
        same = (trainer_row[...] == trainer_ref[me]).astype(f32)
        count = jnp.sum(same, axis=1, keepdims=True)
        scale = 2.0 * (1.0 / (count * CELLS))
        for copy in near:
            copy.wait()
        cut_cube(own_block, y_near, payload, window, north_rows, south_rows, eddies)
        build_stack(payload, stack, hiddens, errors)
        bounds = (0, 5, 10, CX)
        for k in range(INNER):
            gradient(
                scale, weights if k else start, payload, stack, hiddens, slopes, errors, pres,
                now_first, now_last, now_out, grad,
            )

            def send(j, carry):
                to = far_first(column, j)
                pltpu.make_async_remote_copy(
                    grad.at[pl.ds(pl.multiple_of(to * 8, 8), 8)],
                    gathered.at[pl.ds(pl.multiple_of(me * 8, 8), 8)],
                    up_send,
                    up_recv,
                    device_id=device(last_group, to),
                ).start()
                return carry

            lax.fori_loop(0, TILES, send, 0, unroll=4)
            if k == 0:
                for copy in halos:
                    copy.wait()
            evolve(bounds[k], bounds[k + 1], out_ref, padded, y_low, y_high, new_fields, wide_ref)
            whole(grad, up_send).wait()
            if k < INNER - 1:
                whole(weights, down_recv).wait()
        whole(delta, last_recv).wait()

        @pl.when(group == 0)
        def _():
            hand = pltpu.make_async_remote_copy(delta, delta, hand_send, last_recv, device_id={"grp": 1})
            hand.start()
            hand.wait_send()

    @pl.when(group == last_group)
    def _():
        keep = pltpu.make_async_copy(brick, new_fields, load_sem)
        keep.start()

        def greet_owners(j, carry):
            for g in range(OWNERS // TRAINERS):
                pl.semaphore_signal(barrier, 1, device_id=device(g, far_first(column, j)), device_id_type=MESH)
            return carry

        def greet(j, carry):
            pl.semaphore_signal(barrier, 1, device_id=device(last_group, far_first(column, j)), device_id_type=MESH)
            return carry

        lax.fori_loop(0, TRAINERS, greet_owners, 0)
        lax.fori_loop(0, TRAINERS - 1, greet, 0)
        for copy in small:
            copy.wait()
        start_tables()
        own_start = start[pl.ds(pl.multiple_of(column * 8, 8), 8), :]
        square = (OWNERS, OWNERS)
        across = jnp.broadcast_to(trainer_row[...].astype(f32), square)
        diagonal = jnp.where(iota(square, 0) == iota(square, 1), across, 0.0)
        down = jnp.sum(diagonal, axis=1, keepdims=True)
        same = (across == down).astype(f32).astype(bf16)
        running[...] = jnp.zeros_like(running)
        pl.semaphore_wait(barrier, OWNERS + TRAINERS - 1)
        total = jnp.zeros((8, 128), f32)
        for k in range(INNER):
            whole(gathered, up_recv).wait()

            def add(o, total):
                return total + gathered[pl.ds(pl.multiple_of(o * 8, 8), 8), :]

            total = lax.fori_loop(0, OWNERS, add, total, unroll=8)
            if k < INNER - 1:
                if k:
                    whole(answer, down_send).wait()
                for r in range(8):
                    terms = three_terms(gathered[pl.ds(r, OWNERS, stride=8), :])
                    part = sum(jnp.dot(same, term, preferred_element_type=f32) for term in terms)
                    part = running[r] + part
                    running[r] = part
                    answer[pl.ds(r, OWNERS, stride=8), :] = own_start[r : r + 1] - inner_rate * part

                def send(j, carry):
                    to = far_first(column, j)
                    for g in range(OWNERS // TRAINERS):
                        pltpu.make_async_remote_copy(
                            answer.at[pl.ds(pl.multiple_of((g * TRAINERS + to) * 8, 8), 8)],
                            weights.at[pl.ds(pl.multiple_of(column * 8, 8), 8)],
                            down_send,
                            down_recv,
                            device_id=device(g, to),
                        ).start()
                    return carry

                lax.fori_loop(0, TRAINERS, send, 0, unroll=2)
        whole(answer, down_send).wait()
        own = delta.at[pl.ds(pl.multiple_of(column * 8, 8), 8)]
        own[...] = inner_rate * total

        def tell(j, carry):
            to = far_first(column, j)
            for g in (0, last_group):
                pltpu.make_async_remote_copy(own, own, last_send, last_recv, device_id=device(g, to)).start()
            return carry

        lax.fori_loop(0, TRAINERS - 1, tell, 0)
        pltpu.make_async_remote_copy(own, own, last_send, last_recv, device_id=device(0, column)).start()
        others = delta.at[pl.ds(0, (TILES - 1) * 8)]
        whole(others, last_recv).wait()
        hand = pltpu.make_async_remote_copy(delta, delta, hand_send, last_recv, device_id={"grp": 2})
        hand.start()
        whole(delta, last_send).wait()
        whole(others, last_send).wait()
        hand.wait_send()
        keep.wait()

    values = delta[...]
    inverse = lax.rsqrt(jnp.sum(values * values) / NPARAM + norm_epsilon)
    share[...] = inverse * share_of(table_of(delta, 0), table_of(delta, 1), me)


def step_call(sample_block, sample_trainer, closure_out, closure_in, closure_bias, master, brick):
    vmem = pl.BlockSpec(memory_space=pltpu.VMEM)
    hbm = pl.BlockSpec(memory_space=pltpu.HBM)
    dma = pltpu.SemaphoreType.DMA
    operands = (
        sample_block, sample_trainer, closure_out, closure_in.T, closure_bias.reshape(1, CH),
        sample_trainer.reshape(1, OWNERS), master.reshape(135, 128), brick,
    )
    spaces = [pltpu.SMEM] * 3 + [pltpu.VMEM] * 4
    return pl.pallas_call(
        step_kernel,
        out_shape=(
            jax.ShapeDtypeStruct((F, CX, CY, CZ), f32),
            jax.ShapeDtypeStruct((1, 135), f32),
        ),
        in_specs=[hbm] * 8,
        out_specs=(vmem, vmem),
        scratch_shapes=[space(x.shape, x.dtype) for space, x in zip(spaces, operands)]
        + [
            pltpu.VMEM((1024, 256), bf16),
            pltpu.VMEM((F, CX + 2, CY, CZ), f32),
            pltpu.VMEM((F, CX, CZ), f32),
            pltpu.VMEM((F, CX, CZ), f32),
            pltpu.VMEM((2, F, CX, CZ), f32),
            pltpu.VMEM((16, CELLS), bf16),
            pltpu.VMEM((F, 18, 16, 128), f32),
            pltpu.VMEM((F, 16, 128), f32),
            pltpu.VMEM((F, 16, 128), f32),
            pltpu.VMEM((4, 16, 512), f32),
            pltpu.VMEM((2, F, 16, 128), f32),
            pltpu.VMEM((2, F, 16, 128), f32),
            pltpu.VMEM((2, F, 16, 128), f32),
            pltpu.VMEM((KROWS, WIDE), bf16),
            pltpu.VMEM((3 * CH, WIDE), bf16),
            pltpu.VMEM((CH, CELLS), f32),
            pltpu.VMEM((KROWS, WIDE), bf16),
            pltpu.VMEM((CH, CELLS), bf16),
            pltpu.VMEM((CH, KROWS), bf16),
            pltpu.VMEM((CH, KROWS), bf16),
            pltpu.VMEM((80, 3 * CH), bf16),
            pltpu.VMEM((TILES * 8, 128), f32),
            pltpu.VMEM((TILES * 8, 128), f32),
            pltpu.VMEM((TILES * 8, 128), f32),
            pltpu.VMEM((OWNERS * 8, 128), f32),
            pltpu.VMEM((OWNERS * 8, 128), f32),
            pltpu.VMEM((8, OWNERS, 128), f32),
            pltpu.VMEM((TILES * 8, 128), f32),
            dma((7,)),
            dma,
            dma((4,)),
            dma((4,)),
            dma((4,)),
            dma((4,)),
            dma,
            dma,
            dma,
            dma,
            dma,
            dma,
            dma,
        ],
        compiler_params=pltpu.CompilerParams(vmem_limit_bytes=60 * 2**20, has_side_effects=True, collective_id=0),
    )(*operands)


def finish_kernel(made, share, momentum, master, new_fields, new_master, new_momentum, held, in_sems, out_sems):
    into = [pltpu.make_async_copy(made.at[f], held.at[f], in_sems.at[f]) for f in range(F)]
    out = [pltpu.make_async_copy(held.at[f], new_fields.at[f], out_sems.at[f]) for f in range(F)]
    for copy in into:
        copy.start()
    columns = lax.axis_size("gy")
    me = lax.axis_index("grp") * TRAINERS + lax.axis_index("gx") * columns + lax.axis_index("gy")
    begin = me * 135
    row = begin // 128

    def mine(flat):
        rows = [flat[pl.ds(jnp.minimum(row + i, 134), 1), :] for i in range(3)]
        wide = jnp.broadcast_to(jnp.concatenate(rows, axis=1), (8, 384))
        return pltpu.roll(wide, lax.rem(384 - begin % 128, 384), 1)[:1, :135]

    momentum_share = momentum_decay * mine(momentum) + share[...]
    new_momentum[...] = momentum_share
    new_master[...] = mine(master) - outer_rate * momentum_share
    for f in range(F):
        into[f].wait()
        out[f].start()
    for f in range(F):
        out[f].wait()


def finish_call(made, share, momentum, master):
    vmem = pl.BlockSpec(memory_space=pltpu.VMEM)
    hbm = pl.BlockSpec(memory_space=pltpu.HBM)
    part = jax.ShapeDtypeStruct((1, 135), f32)
    return pl.pallas_call(
        finish_kernel,
        out_shape=(jax.ShapeDtypeStruct(made.shape, made.dtype), part, part),
        in_specs=[hbm, vmem, vmem, vmem],
        out_specs=(hbm, vmem, vmem),
        scratch_shapes=[
            pltpu.VMEM(made.shape, f32),
            pltpu.SemaphoreType.DMA((F,)),
            pltpu.SemaphoreType.DMA((F,)),
        ],
        compiler_params=pltpu.CompilerParams(vmem_limit_bytes=60 * 2**20),
    )(made, share, momentum.reshape(135, 128), master.reshape(135, 128))


def on_device(
    fields, closure_in, closure_bias, closure_out, master, momentum, sample_block, sample_trainer
):
    made, share = step_call(
        sample_block, sample_trainer, closure_out, closure_in, closure_bias, master, fields[0]
    )
    new_fields, new_master, new_momentum = finish_call(made, share, momentum, master)
    return (new_fields[None], new_master.reshape(135), new_momentum.reshape(135))


def solution(mesh):
    in_specs = (P("grp", None, "gx", "gy", None), P(), P(), P(), P(), P(), P(), P())
    out_specs = (P("grp", None, "gx", "gy", None), P(("grp", "gx", "gy")), P(("grp", "gx", "gy")))
    return jax.shard_map(
        on_device, mesh=mesh, in_specs=in_specs, out_specs=out_specs, check_vma=False
    )
```

```python
import jax
import jax.numpy as jnp
from jax import lax
from jax.experimental import pallas as pl
from jax.experimental.pallas import tpu as pltpu
from jax.sharding import PartitionSpec as P

F = 5
CH = 64
SUB = 16
CX = 16
CY = 32
CZ = 384
INNER = 3
CELLS = 4096
NPARAM = 17280
FIRST = CH * 27 * F
OWNERS = 96
TRAINERS = 32
TILES = 32
KROWS = 240
BASE = 256
WIDE = CELLS + 2 * BASE
CHUNK = 512

time_step = 0.1
base_viscosity = 0.02
viscosity_gain = 0.2
buoyancy = 0.5
inner_rate = 0.02
outer_rate = 0.01
momentum_decay = 0.9
norm_epsilon = 1e-06
f32 = jnp.float32
MESH = pl.DeviceIdType.MESH
bf16 = jnp.bfloat16
NT = (((1,), (1,)), ((), ()))


def iota(shape, dim):
    return lax.broadcasted_iota(jnp.int32, shape, dim)


def spread_closure(closure_in, closure_bias, wide_ref):
    half = 0.5 * closure_in[...]
    inner = (((0,), (0,)), ((), ()))
    high = half.astype(bf16)
    low = (half - high.astype(f32)).astype(bf16)
    column = iota((F, 256), 1)
    fields = (iota((F, 256), 0) == column // 16 % F) & (column < 240)
    of_high = (fields & (column < 160)).astype(f32).astype(bf16)
    of_low = (fields & (column >= 160)).astype(f32).astype(bf16)
    table = lax.dot_general(high, of_high, inner, preferred_element_type=f32)
    table = table + lax.dot_general(low, of_low, inner, preferred_element_type=f32)
    diagonal = iota((CH, CH), 0) == iota((CH, CH), 1)
    bias = 0.5 * jnp.sum(jnp.where(diagonal, closure_bias[...], 0.0), axis=1, keepdims=True)
    lane = iota((CH, 256), 1)
    for place in range(240, 243):
        term = bias.astype(bf16).astype(f32)
        table = jnp.where(lane == place, term, table)
        bias = bias - term
    table = table.astype(bf16)
    for part in range(8):
        pick = (iota((128, CH), 0) // 16 + part * 8 == iota((128, CH), 1)).astype(f32).astype(bf16)
        rows = jnp.dot(pick, table, preferred_element_type=f32)
        row = iota((128, 256), 0) % 16
        column = iota((128, 256), 1)
        keep = (row == column % 16) | (column >= 240)
        wide_ref[part * 128 : (part + 1) * 128, :] = jnp.where(keep, rows, 0.0).astype(bf16)


def closure(cells, wide_ref, out_ref):
    length = cells.shape[1]
    high = cells.astype(bf16)
    low = (cells - high.astype(f32)).astype(bf16)
    stack = jnp.concatenate([high, low, high, jnp.ones((16, length), bf16)], axis=0)
    total = jnp.zeros((16, length), f32)
    for part in range(8):
        half = jnp.dot(wide_ref[part * 128 : (part + 1) * 128, :], stack, preferred_element_type=f32)
        bent = jnp.tanh(half)
        for k in range(8):
            h = half[k * 16 : (k + 1) * 16]
            t = bent[k * 16 : (k + 1) * 16]
            total = total + out_ref[part * 8 + k] * (h + h * t)
    return viscosity_gain * (jnp.maximum(total, 0.0) + jnp.log1p(jnp.exp(-jnp.abs(total))))


def advance(center, east, west, north, south, upper, lower, eddy):
    viscosity = base_viscosity + eddy
    result = []
    for f in range(F):
        laplacian = east[f] + west[f] + north[f] + south[f] + upper[f] + lower[f] - 6.0 * center[f]
        advection = (
            center[0] * (east[f] - west[f])
            + center[1] * (north[f] - south[f])
            + center[2] * (upper[f] - lower[f])
        )
        value = viscosity * laplacian - 0.5 * advection
        if f == 2:
            value = value + buoyancy * center[3]
        result.append(value)
    return result


def cut(rows, z_block):
    rolled = pltpu.roll(rows, lax.rem(CZ + 1 - z_block * 16, CZ), 1)[:, :128]
    lane = iota(rolled.shape, 1)
    outside = ((lane == 0) & (z_block == 0)) | ((lane == 17) & (z_block == 23))
    return jnp.where(outside, 0.0, rolled)


def own_windows(block, out_ref, padded, wide_ref, window, north_rows, south_rows, eddies):
    upper_half = block // 24 == 1
    z_block = block % 24
    for f in range(F):
        rows = jnp.where(upper_half, padded[f, 1 : CX + 1, 15, :], padded[f, 1 : CX + 1, 16, :])
        rows = cut(rows, z_block)
        south_rows[f] = rows
        north_rows[f] = rows

    def load(x, carry):
        for f in range(F):
            window[f, x] = cut(jnp.where(upper_half, padded[f, x, 16:, :], padded[f, x, :16, :]), z_block)
        return carry

    lax.fori_loop(1, CX + 1, load, 0, unroll=2)

    def quarter(i, carry):
        x0 = i * 4
        cells = jnp.concatenate(
            [jnp.concatenate([window[f, x0 + j + 1] for f in range(F)], axis=0) for j in range(4)], axis=1
        )
        eddies[i] = closure(cells, wide_ref, out_ref)
        return carry

    lax.fori_loop(0, 4, quarter, 0)


def cut_cube(block, y_near, payload, window, north_rows, south_rows, eddies, cube_cells, cube_rows):
    upper_half = block // 24 == 1
    for f in range(F):
        south_rows[f] = jnp.where(upper_half, south_rows[f], y_near[0, f])
        north_rows[f] = jnp.where(upper_half, y_near[1, f], north_rows[f])
    lane = iota((128, 256), 0)
    place = iota((128, 256), 1)
    unfold = (lane - 1 == place % 16).astype(f32).astype(bf16)
    own_row = iota((160, 256), 0) % 16 == iota((160, 256), 1) // 16
    group = iota((16, 160), 1) // 16
    gather = (jnp.where(group < 5, group, group + 3) == iota((16, 160), 0)).astype(f32).astype(bf16)
    row = iota((16, 128), 0)

    def quarter(i, carry):
        eddy = eddies[i]
        for j in range(4):
            x = i * 4 + j
            center = [window[f, x + 1] for f in range(F)]
            east = [window[f, x + 2] for f in range(F)]
            west = [window[f, x] for f in range(F)]
            north = [
                jnp.where(row == 15, north_rows[f, pl.ds(x, 1), :], pltpu.roll(center[f], 15, 0)) for f in range(F)
            ]
            south = [
                jnp.where(row == 0, south_rows[f, pl.ds(x, 1), :], pltpu.roll(center[f], 1, 0)) for f in range(F)
            ]
            upper = [pltpu.roll(center[f], 127, 1) for f in range(F)]
            lower = [pltpu.roll(center[f], 1, 1) for f in range(F)]
            tendency = advance(
                center, east, west, north, south, upper, lower, eddy[:, j * 128 : (j + 1) * 128]
            )
            cube_cells[x] = jnp.concatenate(center + tendency, axis=0).astype(bf16)
        return carry

    lax.fori_loop(0, 4, quarter, 0)
    for x in range(CX):
        flat = jnp.dot(cube_cells[x], unfold, preferred_element_type=f32)
        cube_rows[:, x * 256 : (x + 1) * 256] = jnp.where(own_row, flat, 0.0).astype(bf16)
    payload[...] = jnp.dot(gather, cube_rows[...], preferred_element_type=f32).astype(bf16)


def evolve(begin, end, out_ref, padded, y_low, y_high, new_fields, wide_ref):
    row = iota((CY, CZ), 0)
    lane = iota((CY, CZ), 1)

    def plane(x, carry):
        center = [padded[f, x + 1] for f in range(F)]
        cells = jnp.concatenate(
            [jnp.concatenate([c[h * 16 : (h + 1) * 16] for c in center], axis=0) for h in range(2)], axis=1
        )
        eddy = closure(cells, wide_ref, out_ref)
        eddy = jnp.concatenate([eddy[:, :CZ], eddy[:, CZ:]], axis=0)
        center = [padded[f, x + 1] for f in range(F)]
        east = [padded[f, x + 2] for f in range(F)]
        west = [padded[f, x] for f in range(F)]
        north = [
            jnp.where(row == CY - 1, y_high[f, pl.ds(x, 1), :], pltpu.roll(center[f], CY - 1, 0)) for f in range(F)
        ]
        south = [jnp.where(row == 0, y_low[f, pl.ds(x, 1), :], pltpu.roll(center[f], 1, 0)) for f in range(F)]
        upper = [jnp.where(lane == CZ - 1, 0.0, pltpu.roll(center[f], CZ - 1, 1)) for f in range(F)]
        lower = [jnp.where(lane == 0, 0.0, pltpu.roll(center[f], 1, 1)) for f in range(F)]
        tendency = advance(center, east, west, north, south, upper, lower, eddy)
        for f in range(F):
            new_fields[f, x] = center[f] + time_step * tendency[f]
        return carry

    lax.fori_loop(begin, end, plane, 0)


def shifted(values, y_step, z_step):
    length = values.shape[1]
    offset = 16 * y_step + z_step
    place = iota(values.shape, 1)
    if y_step:
        y = place // 16 % 16 + y_step
        inside = (y >= 0) & (y < 16)
    else:
        z = place % 16 + z_step
        inside = (z >= 0) & (z < 16)
    return jnp.where(inside, pltpu.roll(values, -offset % length, 1), 0.0)


STEPS = (-1, 0, 1)


def nine(values, sign):
    along_z = {s: values if s == 0 else shifted(values, 0, sign * s) for s in STEPS}
    rows = []
    for y_step in STEPS:
        for z_step in STEPS:
            part = along_z[z_step]
            rows.append(part if y_step == 0 else shifted(part, sign * y_step, 0))
    rows.append(jnp.zeros_like(values))
    return jnp.concatenate(rows, axis=0)


def build_stack(payload, stack, hiddens, errors):
    for x_step in STEPS:
        if x_step:
            block = x_step + 1
            ends = (slice(BASE, 2 * BASE), slice(CELLS, CELLS + BASE))
            edge, empty = ends if x_step < 0 else ends[::-1]
            errors[block * 80 : (block + 1) * 80, empty] = jnp.zeros((80, BASE), bf16)
            hiddens[block * CH : (block + 1) * CH, edge] = jnp.zeros((CH, BASE), bf16)
            stack[block * 80 : (block + 1) * 80, edge] = jnp.zeros((80, BASE), bf16)
    for o in range(0, CELLS, CHUNK):
        rows = nine(payload[:, o : o + CHUNK].astype(f32)[:8], 1).astype(bf16)
        for x_step in STEPS:
            at = BASE + o - BASE * x_step
            stack[(x_step + 1) * 80 : (x_step + 2) * 80, at : at + CHUNK] = rows


def table_of(tiles, layer):
    return jnp.concatenate(
        [tiles[layer * 128 : layer * 128 + 64, :], tiles[layer * 128 + 64 : layer * 128 + 128, :]], axis=1
    )


def set_table(tiles, layer, table):
    tiles[layer * 128 : layer * 128 + 64, :] = table[:, :128]
    tiles[layer * 128 + 64 : layer * 128 + 128, :] = table[:, 128:]


def gradient(scale, weights, payload, stack, hiddens, slopes, errors, pres, now_first, now_last, now_out, grad):
    eye = (iota((KROWS, KROWS), 0) == iota((KROWS, KROWS), 1)).astype(f32).astype(bf16)
    now_first[...] = table_of(weights, 0)[:, :KROWS].astype(bf16)
    last = table_of(weights, 1)[:, :KROWS].astype(bf16)
    now_last[...] = last
    turned = lax.dot_general(eye, last, NT, preferred_element_type=f32)
    now_out[...] = jnp.concatenate([turned[b * 80 : (b + 1) * 80] for b in range(3)], axis=1).astype(bf16)
    for i in range(0, CELLS, CHUNK):
        o = BASE + i
        pre = jnp.dot(now_first[...], stack[:, o : o + CHUNK], preferred_element_type=f32)
        sigmoid = 0.5 + 0.5 * jnp.tanh(0.5 * pre)
        hidden = pre * sigmoid
        slopes[:, i : i + CHUNK] = sigmoid + hidden * (1.0 - sigmoid)
        hidden = hidden.astype(bf16)
        for x_step in STEPS:
            at = o - BASE * x_step
            hiddens[(x_step + 1) * CH : (x_step + 2) * CH, at : at + CHUNK] = hidden
    for i in range(0, CELLS, CHUNK):
        o = BASE + i
        parts = jnp.dot(now_out[...], hiddens[:, o : o + CHUNK], preferred_element_type=f32)
        predicted = None
        for z_step in STEPS:
            line = None
            for y_step in STEPS:
                row = ((y_step + 1) * 3 + z_step + 1) * 8
                part = parts[row : row + 8]
                part = part if y_step == 0 else shifted(part, y_step, 0)
                line = part if line is None else line + part
            line = line if z_step == 0 else shifted(line, 0, z_step)
            predicted = line if predicted is None else predicted + line
        targets = payload[:, i : i + CHUNK].astype(f32)[8:]
        error = (scale * (predicted - targets)).astype(bf16).astype(f32)
        rows = nine(error, -1).astype(bf16)
        for x_step in STEPS:
            at = o + BASE * x_step
            errors[(x_step + 1) * 80 : (x_step + 2) * 80, at : at + CHUNK] = rows
    for i in range(0, CELLS, CHUNK):
        o = BASE + i
        back = jnp.dot(now_last[...], errors[:, o : o + CHUNK], preferred_element_type=f32)
        pres[:, i : i + CHUNK] = (back * slopes[:, i : i + CHUNK]).astype(bf16)
    cells = slice(BASE, BASE + CELLS)
    spare = jnp.zeros((CH, 256 - KROWS), f32)
    first = lax.dot_general(pres[...], stack[:, cells], NT, preferred_element_type=f32)
    set_table(grad, 0, jnp.concatenate([first, spare], axis=1))
    last = lax.dot_general(hiddens[CH : 2 * CH, cells], errors[:, cells], NT, preferred_element_type=f32)
    set_table(grad, 1, jnp.concatenate([last, spare], axis=1))


def three_terms(values):
    high = values.astype(bf16)
    rest = values - high.astype(f32)
    middle = rest.astype(bf16)
    return high, middle, (rest - middle.astype(f32)).astype(bf16)


def lane_of(offset, field):
    return offset // 9 * 80 + offset % 9 * 8 + field


def parameter_of(layer):
    lane = iota((1, 256), 1)
    rest = lane % 80
    offset, field = lane // 80 * 9 + rest // 8, rest % 8
    index = offset * F + field if layer == 0 else field * 27 + offset
    return jnp.where((lane < KROWS) & (rest < 72) & (field < F), index, -1)


def one_hot(condition):
    return condition.astype(f32).astype(bf16)


def first_table(flat):
    wide = jnp.concatenate([flat[m : m + CH] for m in range(5)], axis=1)
    unit = iota((CH, 640), 0)
    for bit in range(6):
        wide = jnp.where(unit // 2**bit % 2 == 1, pltpu.roll(wide, 640 - 7 * 2**bit, 1), wide)
    pick = one_hot(iota((256, 256), 0) == parameter_of(0))
    return jnp.dot(wide[:, :256].astype(bf16), pick, preferred_element_type=f32)


def last_table(flat):
    lane = iota((256, 1), 0)
    rest = lane % 80
    row = rest % 8 * 27 + lane // 80 * 9 + rest // 8
    valid = (lane < KROWS) & (rest < 72) & (rest % 8 < F)
    source = jnp.where(valid, 67 + (row + 1) // 2, -1)
    pick = one_hot(iota((256, 135), 1) == source)
    both = jnp.dot(pick, flat.astype(bf16), preferred_element_type=f32)
    mine = jnp.where((row + 1) % 2 == 1, both[:, CH:], both[:, :CH]).astype(bf16)
    eye = one_hot(iota((CH, CH), 0) == iota((CH, CH), 1))
    return lax.dot_general(eye, mine, NT, preferred_element_type=f32)


def share_of(first, last, me):
    of_first = me < CH
    table = jnp.where(of_first, first, last)
    place = iota((135, 1), 0)
    flat = (me - CH) * 135 + place
    row = flat // CH
    lane = jnp.where(of_first, lane_of(place // F, place % F), lane_of(row % 27, row // 27))
    pick = one_hot(iota((135, 256), 1) == lane)
    values = sum(lax.dot_general(term, pick, NT, preferred_element_type=f32) for term in three_terms(table))
    along = iota((CH, 135), 1)
    unit = jnp.where(of_first, me, ((me - CH) * 135 + along) % CH)
    return jnp.sum(jnp.where(iota((CH, 135), 0) == unit, values, 0.0), axis=0, keepdims=True)


def device(group, column):
    columns = lax.axis_size("gy")
    return {"grp": group, "gx": column // columns, "gy": lax.rem(column, columns)}


def far_first(column, j):
    def offset(t):
        return (2 + 3 * t + 3 * (t // 2) + 2 * (t // 3)) % 4

    gx, gy = column // 4, lax.rem(column, 4)
    z = lax.rem(gx // 2 + offset(j // 8), 4)
    y = lax.rem(gx + 1 - lax.rem(j, 2), 2)
    x = lax.rem(gy + offset(lax.rem(j // 2, 4)), 4)
    return (z * 2 + y) * 4 + x


def whole(ref, sem):
    return pltpu.make_async_copy(ref, ref, sem)


def step_kernel(
    block_in, trainer_in, out_in, closure_in_, closure_bias_, trainer_row_, flat_in_, brick,
    new_fields, share,
    block_ref, trainer_ref, out_ref, closure_in, closure_bias, trainer_row, flat_in,
    wide_ref, padded, y_low, y_high, y_send, payload, window, north_rows, south_rows, eddies, x_near_send, y_near_send, y_near,
    cube_cells, cube_rows, stack, hiddens, slopes, errors, pres, now_first, now_last, now_out,
    start, weights, grad, gathered, answer, running, delta,
    small_sems, load_sem, near_send, near_recv, halo_send, halo_recv,
    up_send, up_recv, down_send, down_recv, last_send, last_recv, hand_send,
):
    group = lax.axis_index("grp")
    column = lax.axis_index("gx") * lax.axis_size("gy") + lax.axis_index("gy")
    me = group * TRAINERS + column
    last_group = lax.axis_size("grp") - 1
    barrier = pltpu.get_barrier_semaphore()
    sources = (block_in, trainer_in, out_in, closure_in_, closure_bias_, trainer_row_, flat_in_)
    places_in = (block_ref, trainer_ref, out_ref, closure_in, closure_bias, trainer_row, flat_in)
    small = [
        pltpu.make_async_copy(source, to, small_sems.at[i]) for i, (source, to) in enumerate(zip(sources, places_in))
    ]
    for copy in small:
        copy.start()

    def start_tables():
        flat = flat_in[...]
        set_table(start, 0, first_table(flat))
        set_table(start, 1, last_table(flat))

    @pl.when(group < last_group)
    def _():
        load = pltpu.make_async_copy(brick, padded.at[:, pl.ds(1, CX)], load_sem)
        load.start()
        gx, gy = lax.axis_index("gx"), lax.axis_index("gy")
        gx_size, gy_size = lax.axis_size("gx"), lax.axis_size("gy")
        x_next, x_last = lax.rem(gx + 1, gx_size), lax.rem(gx + gx_size - 1, gx_size)
        y_next, y_last = lax.rem(gy + 1, gy_size), lax.rem(gy + gy_size - 1, gy_size)

        def greet(j, carry):
            pl.semaphore_signal(barrier, 1, device_id=device(last_group, far_first(column, j)), device_id_type=MESH)
            return carry

        lax.fori_loop(0, TRAINERS, greet, 0, unroll=True)
        for to in (x_next, x_last):
            pl.semaphore_signal(barrier, 1, device_id={"gx": to}, device_id_type=MESH)
        for to in (y_next, y_last):
            pl.semaphore_signal(barrier, 1, device_id={"gy": to}, device_id_type=MESH)

        before = lax.rem(group + last_group - 1, last_group)
        pl.semaphore_signal(barrier, 1, device_id={"grp": before}, device_id_type=MESH)

        for copy in small:
            copy.wait()
        spread_closure(closure_in, closure_bias, wide_ref)
        first_owner = group * TRAINERS
        load.wait()
        near = []
        for side, to in enumerate((x_next, x_last)):
            block = block_ref[first_owner + to * gy_size + gy]
            plane = CX if side == 0 else 1
            for f in range(F):
                rows = jnp.where(block // 24 == 1, padded[f, plane, 16:, :], padded[f, plane, :16, :])
                x_near_send[side, f] = cut(rows, block % 24)
            near.append(
                pltpu.make_async_remote_copy(
                    x_near_send.at[side],
                    window.at[:, 0 if side == 0 else CX + 1],
                    near_send.at[side],
                    near_recv.at[side],
                    device_id={"gx": to},
                )
            )
        for side, to in enumerate((y_next, y_last)):
            block = block_ref[first_owner + gx * gy_size + to]
            line = CY - 1 if side == 0 else 0
            for f in range(F):
                rows = padded[f, 1 : CX + 1, line, :]
                y_send[side, f] = rows
                y_near_send[side, f] = cut(rows, block % 24)
            near.append(
                pltpu.make_async_remote_copy(
                    y_near_send.at[side],
                    y_near.at[side],
                    near_send.at[2 + side],
                    near_recv.at[2 + side],
                    device_id={"gy": to},
                )
            )
        own_block = block_ref[me]
        own_windows(own_block, out_ref, padded, wide_ref, window, north_rows, south_rows, eddies)
        pl.semaphore_wait(barrier, TRAINERS + 5)
        halos = [
            pltpu.make_async_remote_copy(
                brick.at[:, CX - 1], padded.at[:, 0], halo_send.at[0], halo_recv.at[0], device_id={"gx": x_next}
            ),
            pltpu.make_async_remote_copy(
                brick.at[:, 0], padded.at[:, CX + 1], halo_send.at[1], halo_recv.at[1], device_id={"gx": x_last}
            ),
            pltpu.make_async_remote_copy(
                y_send.at[0], y_low, halo_send.at[2], halo_recv.at[2], device_id={"gy": y_next}
            ),
            pltpu.make_async_remote_copy(
                y_send.at[1], y_high, halo_send.at[3], halo_recv.at[3], device_id={"gy": y_last}
            ),
        ]
        for copy in near + halos:
            copy.start()
        start_tables()
        same = (trainer_row[...] == trainer_ref[me]).astype(f32)
        count = jnp.sum(same, axis=1, keepdims=True)
        scale = 2.0 * (1.0 / (count * CELLS))
        for copy in near:
            copy.wait()
        cut_cube(own_block, y_near, payload, window, north_rows, south_rows, eddies, cube_cells, cube_rows)
        build_stack(payload, stack, hiddens, errors)
        bounds = (0, 5, 10, CX)
        for k in range(INNER):
            gradient(
                scale, weights if k else start, payload, stack, hiddens, slopes, errors, pres,
                now_first, now_last, now_out, grad,
            )

            def send(j, carry):
                to = far_first(column, j)
                pltpu.make_async_remote_copy(
                    grad.at[pl.ds(pl.multiple_of(to * 8, 8), 8)],
                    gathered.at[pl.ds(pl.multiple_of(me * 8, 8), 8)],
                    up_send,
                    up_recv,
                    device_id=device(last_group, to),
                ).start()
                return carry

            lax.fori_loop(0, TILES, send, 0, unroll=True)
            if k == 0:
                for copy in halos:
                    copy.wait()
            evolve(bounds[k], bounds[k + 1], out_ref, padded, y_low, y_high, new_fields, wide_ref)
            whole(grad, up_send).wait()
            if k < INNER - 1:
                whole(weights, down_recv).wait()
        whole(delta, last_recv).wait()

        @pl.when(group == 0)
        def _():
            hand = pltpu.make_async_remote_copy(delta, delta, hand_send, last_recv, device_id={"grp": 1})
            hand.start()
            hand.wait_send()

    @pl.when(group == last_group)
    def _():
        keep = pltpu.make_async_copy(brick, new_fields, load_sem)
        keep.start()

        def greet_owners(j, carry):
            for g in range(OWNERS // TRAINERS):
                pl.semaphore_signal(barrier, 1, device_id=device(g, far_first(column, j)), device_id_type=MESH)
            return carry

        def greet(j, carry):
            pl.semaphore_signal(barrier, 1, device_id=device(last_group, far_first(column, j)), device_id_type=MESH)
            return carry

        lax.fori_loop(0, TRAINERS, greet_owners, 0, unroll=True)
        lax.fori_loop(0, TRAINERS - 1, greet, 0, unroll=True)
        for copy in small:
            copy.wait()
        start_tables()
        own_start = start[pl.ds(pl.multiple_of(column * 8, 8), 8), :]
        square = (OWNERS, OWNERS)
        across = jnp.broadcast_to(trainer_row[...].astype(f32), square)
        diagonal = jnp.where(iota(square, 0) == iota(square, 1), across, 0.0)
        down = jnp.sum(diagonal, axis=1, keepdims=True)
        same = (across == down).astype(f32).astype(bf16)
        running[...] = jnp.zeros_like(running)
        pl.semaphore_wait(barrier, OWNERS + TRAINERS - 1)
        total = jnp.zeros((8, 128), f32)
        for k in range(INNER):
            whole(gathered, up_recv).wait()

            def add(o, total):
                return total + gathered[pl.ds(pl.multiple_of(o * 8, 8), 8), :]

            total = lax.fori_loop(0, OWNERS, add, total, unroll=8)
            if k < INNER - 1:
                if k:
                    whole(answer, down_send).wait()
                for r in range(8):
                    terms = three_terms(gathered[pl.ds(r, OWNERS, stride=8), :])
                    part = sum(jnp.dot(same, term, preferred_element_type=f32) for term in terms)
                    part = running[r] + part
                    running[r] = part
                    answer[pl.ds(r, OWNERS, stride=8), :] = own_start[r : r + 1] - inner_rate * part

                def send(j, carry):
                    to = far_first(column, j)
                    for g in range(OWNERS // TRAINERS):
                        pltpu.make_async_remote_copy(
                            answer.at[pl.ds(pl.multiple_of((g * TRAINERS + to) * 8, 8), 8)],
                            weights.at[pl.ds(pl.multiple_of(column * 8, 8), 8)],
                            down_send,
                            down_recv,
                            device_id=device(g, to),
                        ).start()
                    return carry

                lax.fori_loop(0, TRAINERS, send, 0, unroll=True)
        whole(answer, down_send).wait()
        own = delta.at[pl.ds(pl.multiple_of(column * 8, 8), 8)]
        own[...] = inner_rate * total

        def tell(j, carry):
            to = far_first(column, j)
            for g in (0, last_group):
                pltpu.make_async_remote_copy(own, own, last_send, last_recv, device_id=device(g, to)).start()
            return carry

        lax.fori_loop(0, TRAINERS - 1, tell, 0, unroll=True)
        pltpu.make_async_remote_copy(own, own, last_send, last_recv, device_id=device(0, column)).start()
        others = delta.at[pl.ds(0, (TILES - 1) * 8)]
        whole(others, last_recv).wait()
        hand = pltpu.make_async_remote_copy(delta, delta, hand_send, last_recv, device_id={"grp": 2})
        hand.start()
        whole(delta, last_send).wait()
        whole(others, last_send).wait()
        hand.wait_send()
        keep.wait()

    values = delta[...]
    inverse = lax.rsqrt(jnp.sum(values * values) / NPARAM + norm_epsilon)
    share[...] = inverse * share_of(table_of(delta, 0), table_of(delta, 1), me)


def step_call(sample_block, sample_trainer, closure_out, closure_in, closure_bias, master, brick):
    vmem = pl.BlockSpec(memory_space=pltpu.VMEM)
    hbm = pl.BlockSpec(memory_space=pltpu.HBM)
    dma = pltpu.SemaphoreType.DMA
    operands = (
        sample_block, sample_trainer, closure_out, closure_in.T, closure_bias.reshape(1, CH),
        sample_trainer.reshape(1, OWNERS), master.reshape(135, 128), brick,
    )
    operands = [pltpu.with_memory_space_constraint(x, pltpu.HBM) for x in operands]
    spaces = [pltpu.SMEM] * 3 + [pltpu.VMEM] * 4
    return pl.pallas_call(
        step_kernel,
        out_shape=(
            jax.ShapeDtypeStruct((F, CX, CY, CZ), f32),
            jax.ShapeDtypeStruct((1, 135), f32),
        ),
        in_specs=[hbm] * 8,
        out_specs=(vmem, vmem),
        scratch_shapes=[space(x.shape, x.dtype) for space, x in zip(spaces, operands)]
        + [
            pltpu.VMEM((1024, 256), bf16),
            pltpu.VMEM((F, CX + 2, CY, CZ), f32),
            pltpu.VMEM((F, CX, CZ), f32),
            pltpu.VMEM((F, CX, CZ), f32),
            pltpu.VMEM((2, F, CX, CZ), f32),
            pltpu.VMEM((16, CELLS), bf16),
            pltpu.VMEM((F, 18, 16, 128), f32),
            pltpu.VMEM((F, 16, 128), f32),
            pltpu.VMEM((F, 16, 128), f32),
            pltpu.VMEM((4, 16, 512), f32),
            pltpu.VMEM((2, F, 16, 128), f32),
            pltpu.VMEM((2, F, 16, 128), f32),
            pltpu.VMEM((2, F, 16, 128), f32),
            pltpu.VMEM((CX, 160, 128), bf16),
            pltpu.VMEM((160, CELLS), bf16),
            pltpu.VMEM((KROWS, WIDE), bf16),
            pltpu.VMEM((3 * CH, WIDE), bf16),
            pltpu.VMEM((CH, CELLS), f32),
            pltpu.VMEM((KROWS, WIDE), bf16),
            pltpu.VMEM((CH, CELLS), bf16),
            pltpu.VMEM((CH, KROWS), bf16),
            pltpu.VMEM((CH, KROWS), bf16),
            pltpu.VMEM((80, 3 * CH), bf16),
            pltpu.VMEM((TILES * 8, 128), f32),
            pltpu.VMEM((TILES * 8, 128), f32),
            pltpu.VMEM((TILES * 8, 128), f32),
            pltpu.VMEM((OWNERS * 8, 128), f32),
            pltpu.VMEM((OWNERS * 8, 128), f32),
            pltpu.VMEM((8, OWNERS, 128), f32),
            pltpu.VMEM((TILES * 8, 128), f32),
            dma((7,)),
            dma,
            dma((4,)),
            dma((4,)),
            dma((4,)),
            dma((4,)),
            dma,
            dma,
            dma,
            dma,
            dma,
            dma,
            dma,
        ],
        compiler_params=pltpu.CompilerParams(vmem_limit_bytes=50 * 2**20, has_side_effects=True, collective_id=0),
    )(*operands)


def finish_kernel(made, share, momentum, master, new_fields, new_master, new_momentum, in_sems, out_sems):
    out = [pltpu.make_async_copy(made.at[f], new_fields.at[f], out_sems.at[f]) for f in range(F)]
    columns = lax.axis_size("gy")
    me = lax.axis_index("grp") * TRAINERS + lax.axis_index("gx") * columns + lax.axis_index("gy")
    begin = me * 135
    row = begin // 128

    def mine(flat):
        rows = [flat[pl.ds(jnp.minimum(row + i, 134), 1), :] for i in range(3)]
        wide = jnp.broadcast_to(jnp.concatenate(rows, axis=1), (8, 384))
        return pltpu.roll(wide, lax.rem(384 - begin % 128, 384), 1)[:1, :135]

    momentum_share = momentum_decay * mine(momentum) + share[...]
    new_momentum[...] = momentum_share
    new_master[...] = mine(master) - outer_rate * momentum_share
    for f in range(F):
        out[f].start()
    for f in range(F):
        out[f].wait()


def finish_call(made, share, momentum, master):
    vmem = pl.BlockSpec(memory_space=pltpu.VMEM)
    hbm = pl.BlockSpec(memory_space=pltpu.HBM)
    part = jax.ShapeDtypeStruct((1, 135), f32)
    return pl.pallas_call(
        finish_kernel,
        out_shape=(jax.ShapeDtypeStruct(made.shape, made.dtype), part, part),
        in_specs=[vmem, vmem, vmem, vmem],
        out_specs=(hbm, vmem, vmem),
        scratch_shapes=[
            pltpu.SemaphoreType.DMA((F,)),
            pltpu.SemaphoreType.DMA((F,)),
        ],
        compiler_params=pltpu.CompilerParams(vmem_limit_bytes=6 * 2**20),
    )(made, share, momentum.reshape(135, 128), master.reshape(135, 128))


def on_device(
    fields, closure_in, closure_bias, closure_out, master, momentum, sample_block, sample_trainer
):
    made, share = step_call(
        sample_block, sample_trainer, closure_out, closure_in, closure_bias, master, fields[0]
    )
    new_fields, new_master, new_momentum = finish_call(made, share, momentum, master)
    return (new_fields[None], new_master.reshape(135), new_momentum.reshape(135))


def solution(mesh):
    in_specs = (P("grp", None, "gx", "gy", None), P(), P(), P(), P(), P(), P(), P())
    out_specs = (P("grp", None, "gx", "gy", None), P(("grp", "gx", "gy")), P(("grp", "gx", "gy")))
    return jax.shard_map(
        on_device, mesh=mesh, in_specs=in_specs, out_specs=out_specs, check_vma=False
    )
```

```python
import jax
import jax.numpy as jnp
from jax import lax
from jax.experimental import pallas as pl
from jax.experimental.pallas import tpu as pltpu
from jax.sharding import PartitionSpec as P

F = 5
CH = 64
SUB = 16
CX = 16
CY = 32
CZ = 384
INNER = 3
CELLS = 4096
NPARAM = 17280
FIRST = CH * 27 * F
OWNERS = 96
TRAINERS = 32
TILES = 32
KROWS = 240
BASE = 256
WIDE = CELLS + 2 * BASE
CHUNK = 512

time_step = 0.1
base_viscosity = 0.02
viscosity_gain = 0.2
buoyancy = 0.5
inner_rate = 0.02
outer_rate = 0.01
momentum_decay = 0.9
norm_epsilon = 1e-06
f32 = jnp.float32
MESH = pl.DeviceIdType.MESH
bf16 = jnp.bfloat16
NT = (((1,), (1,)), ((), ()))


def iota(shape, dim):
    return lax.broadcasted_iota(jnp.int32, shape, dim)


def spread_closure(closure_in, closure_bias, wide_ref):
    half = 0.5 * closure_in[...]
    inner = (((0,), (0,)), ((), ()))
    high = half.astype(bf16)
    low = (half - high.astype(f32)).astype(bf16)
    column = iota((F, 256), 1)
    fields = (iota((F, 256), 0) == column // 16 % F) & (column < 240)
    of_high = (fields & (column < 160)).astype(f32).astype(bf16)
    of_low = (fields & (column >= 160)).astype(f32).astype(bf16)
    table = lax.dot_general(high, of_high, inner, preferred_element_type=f32)
    table = table + lax.dot_general(low, of_low, inner, preferred_element_type=f32)
    diagonal = iota((CH, CH), 0) == iota((CH, CH), 1)
    bias = 0.5 * jnp.sum(jnp.where(diagonal, closure_bias[...], 0.0), axis=1, keepdims=True)
    lane = iota((CH, 256), 1)
    for place in range(240, 243):
        term = bias.astype(bf16).astype(f32)
        table = jnp.where(lane == place, term, table)
        bias = bias - term
    table = table.astype(bf16)
    for part in range(8):
        pick = (iota((128, CH), 0) // 16 + part * 8 == iota((128, CH), 1)).astype(f32).astype(bf16)
        rows = jnp.dot(pick, table, preferred_element_type=f32)
        row = iota((128, 256), 0) % 16
        column = iota((128, 256), 1)
        keep = (row == column % 16) | (column >= 240)
        wide_ref[part * 128 : (part + 1) * 128, :] = jnp.where(keep, rows, 0.0).astype(bf16)


def closure(cells, wide_ref, out_ref):
    length = cells.shape[1]
    high = cells.astype(bf16)
    low = (cells - high.astype(f32)).astype(bf16)
    stack = jnp.concatenate([high, low, high, jnp.ones((16, length), bf16)], axis=0)
    total = jnp.zeros((16, length), f32)
    for part in range(8):
        half = jnp.dot(wide_ref[part * 128 : (part + 1) * 128, :], stack, preferred_element_type=f32)
        bent = jnp.tanh(half)
        for k in range(8):
            h = half[k * 16 : (k + 1) * 16]
            t = bent[k * 16 : (k + 1) * 16]
            total = total + out_ref[part * 8 + k] * (h + h * t)
    return viscosity_gain * (jnp.maximum(total, 0.0) + jnp.log1p(jnp.exp(-jnp.abs(total))))


def advance(center, east, west, north, south, upper, lower, eddy):
    viscosity = base_viscosity + eddy
    result = []
    for f in range(F):
        laplacian = east[f] + west[f] + north[f] + south[f] + upper[f] + lower[f] - 6.0 * center[f]
        advection = (
            center[0] * (east[f] - west[f])
            + center[1] * (north[f] - south[f])
            + center[2] * (upper[f] - lower[f])
        )
        value = viscosity * laplacian - 0.5 * advection
        if f == 2:
            value = value + buoyancy * center[3]
        result.append(value)
    return result


def cut(rows, z_block):
    rolled = pltpu.roll(rows, lax.rem(CZ + 1 - z_block * 16, CZ), 1)[:, :128]
    lane = iota(rolled.shape, 1)
    outside = ((lane == 0) & (z_block == 0)) | ((lane == 17) & (z_block == 23))
    return jnp.where(outside, 0.0, rolled)


def own_windows(block, out_ref, padded, wide_ref, window, north_rows, south_rows, eddies):
    upper_half = block // 24 == 1
    z_block = block % 24
    for f in range(F):
        rows = jnp.where(upper_half, padded[f, 1 : CX + 1, 15, :], padded[f, 1 : CX + 1, 16, :])
        rows = cut(rows, z_block)
        south_rows[f] = rows
        north_rows[f] = rows

    def load(x, carry):
        for f in range(F):
            window[f, x] = cut(jnp.where(upper_half, padded[f, x, 16:, :], padded[f, x, :16, :]), z_block)
        return carry

    lax.fori_loop(1, CX + 1, load, 0, unroll=2)

    def quarter(i, carry):
        x0 = i * 4
        cells = jnp.concatenate(
            [jnp.concatenate([window[f, x0 + j + 1] for f in range(F)], axis=0) for j in range(4)], axis=1
        )
        eddies[i] = closure(cells, wide_ref, out_ref)
        return carry

    lax.fori_loop(0, 4, quarter, 0)


def cut_cube(block, y_near, payload, window, north_rows, south_rows, eddies, cube_cells, cube_rows):
    upper_half = block // 24 == 1
    for f in range(F):
        south_rows[f] = jnp.where(upper_half, south_rows[f], y_near[0, f])
        north_rows[f] = jnp.where(upper_half, y_near[1, f], north_rows[f])
    lane = iota((128, 256), 0)
    place = iota((128, 256), 1)
    unfold = (lane - 1 == place % 16).astype(f32).astype(bf16)
    own_row = iota((160, 256), 0) % 16 == iota((160, 256), 1) // 16
    group = iota((16, 160), 1) // 16
    gather = (jnp.where(group < 5, group, group + 3) == iota((16, 160), 0)).astype(f32).astype(bf16)
    row = iota((16, 128), 0)

    def quarter(i, carry):
        eddy = eddies[i]
        for j in range(4):
            x = i * 4 + j
            center = [window[f, x + 1] for f in range(F)]
            east = [window[f, x + 2] for f in range(F)]
            west = [window[f, x] for f in range(F)]
            north = [
                jnp.where(row == 15, north_rows[f, pl.ds(x, 1), :], pltpu.roll(center[f], 15, 0)) for f in range(F)
            ]
            south = [
                jnp.where(row == 0, south_rows[f, pl.ds(x, 1), :], pltpu.roll(center[f], 1, 0)) for f in range(F)
            ]
            upper = [pltpu.roll(center[f], 127, 1) for f in range(F)]
            lower = [pltpu.roll(center[f], 1, 1) for f in range(F)]
            tendency = advance(
                center, east, west, north, south, upper, lower, eddy[:, j * 128 : (j + 1) * 128]
            )
            cube_cells[x] = jnp.concatenate(center + tendency, axis=0).astype(bf16)
        return carry

    lax.fori_loop(0, 4, quarter, 0)
    for x in range(CX):
        flat = jnp.dot(cube_cells[x], unfold, preferred_element_type=f32)
        cube_rows[:, x * 256 : (x + 1) * 256] = jnp.where(own_row, flat, 0.0).astype(bf16)
    payload[...] = jnp.dot(gather, cube_rows[...], preferred_element_type=f32).astype(bf16)


def evolve(begin, end, out_ref, padded, y_low, y_high, new_fields, wide_ref):
    row = iota((CY, CZ), 0)
    lane = iota((CY, CZ), 1)

    def plane(x, carry):
        center = [padded[f, x + 1] for f in range(F)]
        cells = jnp.concatenate(
            [jnp.concatenate([c[h * 16 : (h + 1) * 16] for c in center], axis=0) for h in range(2)], axis=1
        )
        eddy = closure(cells, wide_ref, out_ref)
        eddy = jnp.concatenate([eddy[:, :CZ], eddy[:, CZ:]], axis=0)
        center = [padded[f, x + 1] for f in range(F)]
        east = [padded[f, x + 2] for f in range(F)]
        west = [padded[f, x] for f in range(F)]
        north = [
            jnp.where(row == CY - 1, y_high[f, pl.ds(x, 1), :], pltpu.roll(center[f], CY - 1, 0)) for f in range(F)
        ]
        south = [jnp.where(row == 0, y_low[f, pl.ds(x, 1), :], pltpu.roll(center[f], 1, 0)) for f in range(F)]
        upper = [jnp.where(lane == CZ - 1, 0.0, pltpu.roll(center[f], CZ - 1, 1)) for f in range(F)]
        lower = [jnp.where(lane == 0, 0.0, pltpu.roll(center[f], 1, 1)) for f in range(F)]
        tendency = advance(center, east, west, north, south, upper, lower, eddy)
        for f in range(F):
            new_fields[f, x] = center[f] + time_step * tendency[f]
        return carry

    lax.fori_loop(begin, end, plane, 0)


def shifted(values, y_step, z_step):
    length = values.shape[1]
    offset = 16 * y_step + z_step
    place = iota(values.shape, 1)
    if y_step:
        y = place // 16 % 16 + y_step
        inside = (y >= 0) & (y < 16)
    else:
        z = place % 16 + z_step
        inside = (z >= 0) & (z < 16)
    return jnp.where(inside, pltpu.roll(values, -offset % length, 1), 0.0)


STEPS = (-1, 0, 1)


def nine(values, sign):
    along_z = {s: values if s == 0 else shifted(values, 0, sign * s) for s in STEPS}
    rows = []
    for y_step in STEPS:
        for z_step in STEPS:
            part = along_z[z_step]
            rows.append(part if y_step == 0 else shifted(part, sign * y_step, 0))
    rows.append(jnp.zeros_like(values))
    return jnp.concatenate(rows, axis=0)


def build_stack(payload, stack, hiddens, errors):
    for x_step in STEPS:
        if x_step:
            block = x_step + 1
            ends = (slice(BASE, 2 * BASE), slice(CELLS, CELLS + BASE))
            edge, empty = ends if x_step < 0 else ends[::-1]
            errors[block * 80 : (block + 1) * 80, empty] = jnp.zeros((80, BASE), bf16)
            hiddens[block * CH : (block + 1) * CH, edge] = jnp.zeros((CH, BASE), bf16)
            stack[block * 80 : (block + 1) * 80, edge] = jnp.zeros((80, BASE), bf16)
    for o in range(0, CELLS, CHUNK):
        rows = nine(payload[:, o : o + CHUNK].astype(f32)[:8], 1).astype(bf16)
        for x_step in STEPS:
            at = BASE + o - BASE * x_step
            stack[(x_step + 1) * 80 : (x_step + 2) * 80, at : at + CHUNK] = rows


def table_of(tiles, layer):
    return jnp.concatenate(
        [tiles[layer * 128 : layer * 128 + 64, :], tiles[layer * 128 + 64 : layer * 128 + 128, :]], axis=1
    )


def set_table(tiles, layer, table):
    tiles[layer * 128 : layer * 128 + 64, :] = table[:, :128]
    tiles[layer * 128 + 64 : layer * 128 + 128, :] = table[:, 128:]


def gradient(scale, weights, payload, stack, hiddens, slopes, errors, pres, now_first, now_last, now_out, grad, send):
    eye = (iota((KROWS, KROWS), 0) == iota((KROWS, KROWS), 1)).astype(f32).astype(bf16)
    now_first[...] = table_of(weights, 0)[:, :KROWS].astype(bf16)
    last = table_of(weights, 1)[:, :KROWS].astype(bf16)
    now_last[...] = last
    turned = lax.dot_general(eye, last, NT, preferred_element_type=f32)
    now_out[...] = jnp.concatenate([turned[b * 80 : (b + 1) * 80] for b in range(3)], axis=1).astype(bf16)
    for i in range(0, CELLS, CHUNK):
        o = BASE + i
        pre = jnp.dot(now_first[...], stack[:, o : o + CHUNK], preferred_element_type=f32)
        sigmoid = 0.5 + 0.5 * jnp.tanh(0.5 * pre)
        hidden = pre * sigmoid
        slopes[:, i : i + CHUNK] = sigmoid + hidden * (1.0 - sigmoid)
        hidden = hidden.astype(bf16)
        for x_step in STEPS:
            at = o - BASE * x_step
            hiddens[(x_step + 1) * CH : (x_step + 2) * CH, at : at + CHUNK] = hidden
    for i in range(0, CELLS, CHUNK):
        o = BASE + i
        parts = jnp.dot(now_out[...], hiddens[:, o : o + CHUNK], preferred_element_type=f32)
        predicted = None
        for z_step in STEPS:
            line = None
            for y_step in STEPS:
                row = ((y_step + 1) * 3 + z_step + 1) * 8
                part = parts[row : row + 8]
                part = part if y_step == 0 else shifted(part, y_step, 0)
                line = part if line is None else line + part
            line = line if z_step == 0 else shifted(line, 0, z_step)
            predicted = line if predicted is None else predicted + line
        targets = payload[:, i : i + CHUNK].astype(f32)[8:]
        error = (scale * (predicted - targets)).astype(bf16).astype(f32)
        rows = nine(error, -1).astype(bf16)
        for x_step in STEPS:
            at = o + BASE * x_step
            errors[(x_step + 1) * 80 : (x_step + 2) * 80, at : at + CHUNK] = rows
    cells = slice(BASE, BASE + CELLS)
    spare = jnp.zeros((CH, 256 - KROWS), f32)
    for i in range(0, CELLS, CHUNK):
        o = BASE + i
        back = jnp.dot(now_last[...], errors[:, o : o + CHUNK], preferred_element_type=f32)
        pres[:, i : i + CHUNK] = (back * slopes[:, i : i + CHUNK]).astype(bf16)
    first = lax.dot_general(pres[...], stack[:, cells], NT, preferred_element_type=f32)
    set_table(grad, 0, jnp.concatenate([first, spare], axis=1))
    last = lax.dot_general(hiddens[CH : 2 * CH, cells], errors[:, cells], NT, preferred_element_type=f32)
    set_table(grad, 1, jnp.concatenate([last, spare], axis=1))
    send()


def three_terms(values):
    high = values.astype(bf16)
    rest = values - high.astype(f32)
    middle = rest.astype(bf16)
    return high, middle, (rest - middle.astype(f32)).astype(bf16)


def lane_of(offset, field):
    return offset // 9 * 80 + offset % 9 * 8 + field


def parameter_of(layer):
    lane = iota((1, 256), 1)
    rest = lane % 80
    offset, field = lane // 80 * 9 + rest // 8, rest % 8
    index = offset * F + field if layer == 0 else field * 27 + offset
    return jnp.where((lane < KROWS) & (rest < 72) & (field < F), index, -1)


def one_hot(condition):
    return condition.astype(f32).astype(bf16)


def first_table(flat):
    wide = jnp.concatenate([flat[m : m + CH] for m in range(5)], axis=1)
    unit = iota((CH, 640), 0)
    for bit in range(6):
        wide = jnp.where(unit // 2**bit % 2 == 1, pltpu.roll(wide, 640 - 7 * 2**bit, 1), wide)
    pick = one_hot(iota((256, 256), 0) == parameter_of(0))
    return jnp.dot(wide[:, :256].astype(bf16), pick, preferred_element_type=f32)


def last_table(flat):
    lane = iota((256, 1), 0)
    rest = lane % 80
    row = rest % 8 * 27 + lane // 80 * 9 + rest // 8
    valid = (lane < KROWS) & (rest < 72) & (rest % 8 < F)
    source = jnp.where(valid, 67 + (row + 1) // 2, -1)
    pick = one_hot(iota((256, 135), 1) == source)
    both = jnp.dot(pick, flat.astype(bf16), preferred_element_type=f32)
    mine = jnp.where((row + 1) % 2 == 1, both[:, CH:], both[:, :CH]).astype(bf16)
    eye = one_hot(iota((CH, CH), 0) == iota((CH, CH), 1))
    return lax.dot_general(eye, mine, NT, preferred_element_type=f32)


def share_map(me, share_pick, share_unit):
    of_first = me < CH
    place = iota((144, 1), 0)
    row = ((me - CH) * 135 + place) // CH
    lane = jnp.where(of_first, lane_of(place // F, place % F), lane_of(row % 27, row // 27))
    share_pick[...] = one_hot((iota((144, 256), 1) == lane) & (place < 135))
    along = iota((CH, 144), 1)
    unit = jnp.where(of_first, me, ((me - CH) * 135 + along) % CH)
    share_unit[...] = (iota((CH, 144), 0) == unit).astype(f32)


def share_of(table, share_pick, share_unit):
    values = sum(lax.dot_general(term, share_pick[...], NT, preferred_element_type=f32) for term in three_terms(table))
    return jnp.sum(values * share_unit[...], axis=0, keepdims=True)[:, :135]


def device(group, column):
    columns = lax.axis_size("gy")
    return {"grp": group, "gx": column // columns, "gy": lax.rem(column, columns)}


def far_first(column, j):
    def offset(t):
        return (2 + 3 * t + 3 * (t // 2) + 2 * (t // 3)) % 4

    gx, gy = column // 4, lax.rem(column, 4)
    z = lax.rem(gx // 2 + offset(j // 8), 4)
    y = lax.rem(gx + 1 - lax.rem(j, 2), 2)
    x = lax.rem(gy + offset(lax.rem(j // 2, 4)), 4)
    return (z * 2 + y) * 4 + x


def whole(ref, sem):
    return pltpu.make_async_copy(ref, ref, sem)


def step_kernel(
    block_in, trainer_in, out_in, closure_in_, closure_bias_, trainer_row_, flat_in_, brick,
    new_fields, share,
    block_ref, trainer_ref, out_ref, closure_in, closure_bias, trainer_row, flat_in,
    wide_ref, padded, y_low, y_high, y_send, payload, window, north_rows, south_rows, eddies, x_near_send, y_near_send, y_near,
    cube_cells, cube_rows, stack, hiddens, slopes, errors, pres, now_first, now_last, now_out,
    start, weights, grad, gathered, answer, running, delta, share_pick, share_unit,
    small_sems, load_sem, near_send, near_recv, halo_send, halo_recv,
    up_send, up_recv, down_send, down_recv, last_send, last_recv, hand_send,
):
    group = lax.axis_index("grp")
    column = lax.axis_index("gx") * lax.axis_size("gy") + lax.axis_index("gy")
    me = group * TRAINERS + column
    last_group = lax.axis_size("grp") - 1
    barrier = pltpu.get_barrier_semaphore()
    sources = (block_in, trainer_in, out_in, closure_in_, closure_bias_, trainer_row_, flat_in_)
    places_in = (block_ref, trainer_ref, out_ref, closure_in, closure_bias, trainer_row, flat_in)
    small = [
        pltpu.make_async_copy(source, to, small_sems.at[i]) for i, (source, to) in enumerate(zip(sources, places_in))
    ]
    for copy in small:
        copy.start()

    def start_tables():
        flat = flat_in[...]
        set_table(start, 0, first_table(flat))
        set_table(start, 1, last_table(flat))
        share_map(me, share_pick, share_unit)

    @pl.when(group < last_group)
    def _():
        load = pltpu.make_async_copy(brick, padded.at[:, pl.ds(1, CX)], load_sem)
        load.start()
        gx, gy = lax.axis_index("gx"), lax.axis_index("gy")
        gx_size, gy_size = lax.axis_size("gx"), lax.axis_size("gy")
        x_next, x_last = lax.rem(gx + 1, gx_size), lax.rem(gx + gx_size - 1, gx_size)
        y_next, y_last = lax.rem(gy + 1, gy_size), lax.rem(gy + gy_size - 1, gy_size)

        def greet(j, carry):
            pl.semaphore_signal(barrier, 1, device_id=device(last_group, far_first(column, j)), device_id_type=MESH)
            return carry

        lax.fori_loop(0, TRAINERS, greet, 0, unroll=True)
        for to in (x_next, x_last):
            pl.semaphore_signal(barrier, 1, device_id={"gx": to}, device_id_type=MESH)
        for to in (y_next, y_last):
            pl.semaphore_signal(barrier, 1, device_id={"gy": to}, device_id_type=MESH)

        before = lax.rem(group + last_group - 1, last_group)
        pl.semaphore_signal(barrier, 1, device_id={"grp": before}, device_id_type=MESH)

        for copy in small:
            copy.wait()
        spread_closure(closure_in, closure_bias, wide_ref)
        first_owner = group * TRAINERS
        load.wait()
        near = []
        for side, to in enumerate((x_next, x_last)):
            block = block_ref[first_owner + to * gy_size + gy]
            plane = CX if side == 0 else 1
            for f in range(F):
                rows = jnp.where(block // 24 == 1, padded[f, plane, 16:, :], padded[f, plane, :16, :])
                x_near_send[side, f] = cut(rows, block % 24)
            near.append(
                pltpu.make_async_remote_copy(
                    x_near_send.at[side],
                    window.at[:, 0 if side == 0 else CX + 1],
                    near_send.at[side],
                    near_recv.at[side],
                    device_id={"gx": to},
                )
            )
        for side, to in enumerate((y_next, y_last)):
            block = block_ref[first_owner + gx * gy_size + to]
            line = CY - 1 if side == 0 else 0
            for f in range(F):
                rows = padded[f, 1 : CX + 1, line, :]
                y_send[side, f] = rows
                y_near_send[side, f] = cut(rows, block % 24)
            near.append(
                pltpu.make_async_remote_copy(
                    y_near_send.at[side],
                    y_near.at[side],
                    near_send.at[2 + side],
                    near_recv.at[2 + side],
                    device_id={"gy": to},
                )
            )
        own_block = block_ref[me]
        own_windows(own_block, out_ref, padded, wide_ref, window, north_rows, south_rows, eddies)
        pl.semaphore_wait(barrier, TRAINERS + 5)
        halos = [
            pltpu.make_async_remote_copy(
                brick.at[:, CX - 1], padded.at[:, 0], halo_send.at[0], halo_recv.at[0], device_id={"gx": x_next}
            ),
            pltpu.make_async_remote_copy(
                brick.at[:, 0], padded.at[:, CX + 1], halo_send.at[1], halo_recv.at[1], device_id={"gx": x_last}
            ),
            pltpu.make_async_remote_copy(
                y_send.at[0], y_low, halo_send.at[2], halo_recv.at[2], device_id={"gy": y_next}
            ),
            pltpu.make_async_remote_copy(
                y_send.at[1], y_high, halo_send.at[3], halo_recv.at[3], device_id={"gy": y_last}
            ),
        ]
        for copy in near:
            copy.start()
        start_tables()
        same = (trainer_row[...] == trainer_ref[me]).astype(f32)
        count = jnp.sum(same, axis=1, keepdims=True)
        scale = 2.0 * (1.0 / (count * CELLS))
        for copy in near:
            copy.wait()
        cut_cube(own_block, y_near, payload, window, north_rows, south_rows, eddies, cube_cells, cube_rows)
        build_stack(payload, stack, hiddens, errors)
        bounds = (0, 0, 8, CX)

        def send_layer():
            for j in range(TILES):
                to = far_first(column, j)
                pltpu.make_async_remote_copy(
                    grad.at[pl.ds(pl.multiple_of(to * 8, 8), 8)],
                    gathered.at[pl.ds(pl.multiple_of(me * 8, 8), 8)],
                    up_send,
                    up_recv,
                    device_id=device(last_group, to),
                ).start()

        for k in range(INNER):
            gradient(
                scale, weights if k else start, payload, stack, hiddens, slopes, errors, pres,
                now_first, now_last, now_out, grad, send_layer,
            )
            if k == 0:
                for copy in halos:
                    copy.start()
            if k == 1:
                for copy in halos:
                    copy.wait()
            if k:
                evolve(bounds[k], bounds[k + 1], out_ref, padded, y_low, y_high, new_fields, wide_ref)
            whole(grad, up_send).wait()
            if k < INNER - 1:
                whole(weights, down_recv).wait()
        whole(delta, last_recv).wait()

        @pl.when(group == 0)
        def _():
            hand = pltpu.make_async_remote_copy(delta, delta, hand_send, last_recv, device_id={"grp": 1})
            hand.start()
            hand.wait_send()

    @pl.when(group == last_group)
    def _():
        keep = pltpu.make_async_copy(brick, new_fields, load_sem)
        keep.start()

        def greet_owners(j, carry):
            for g in range(OWNERS // TRAINERS):
                pl.semaphore_signal(barrier, 1, device_id=device(g, far_first(column, j)), device_id_type=MESH)
            return carry

        def greet(j, carry):
            pl.semaphore_signal(barrier, 1, device_id=device(last_group, far_first(column, j)), device_id_type=MESH)
            return carry

        lax.fori_loop(0, TRAINERS, greet_owners, 0, unroll=True)
        lax.fori_loop(0, TRAINERS - 1, greet, 0, unroll=True)
        for copy in small:
            copy.wait()
        start_tables()
        own_start = start[pl.ds(pl.multiple_of(column * 8, 8), 8), :]
        square = (OWNERS, OWNERS)
        across = jnp.broadcast_to(trainer_row[...].astype(f32), square)
        diagonal = jnp.where(iota(square, 0) == iota(square, 1), across, 0.0)
        down = jnp.sum(diagonal, axis=1, keepdims=True)
        same = jnp.concatenate([(across == down).astype(f32), jnp.ones((8, OWNERS), f32)], axis=0).astype(bf16)
        ones = jnp.ones((8, OWNERS), bf16)
        running[...] = jnp.zeros_like(running)

        def summed(rows):
            wide = jnp.concatenate([gathered[pl.ds(r, OWNERS, stride=8), :] for r in range(8)], axis=1)
            return sum(jnp.dot(rows, term, preferred_element_type=f32) for term in three_terms(wide))

        pl.semaphore_wait(barrier, OWNERS + TRAINERS - 1)
        for k in range(INNER):
            whole(gathered, up_recv).wait()
            if k < INNER - 1:
                if k:
                    whole(answer, down_send).wait()
                part = running[...] + summed(same)
                running[...] = part
                for r in range(8):
                    lanes = slice(r * 128, (r + 1) * 128)
                    answer[pl.ds(r, OWNERS, stride=8), :] = own_start[r : r + 1] - inner_rate * part[:OWNERS, lanes]

                def send(j, carry):
                    to = far_first(column, j)
                    for g in range(OWNERS // TRAINERS):
                        pltpu.make_async_remote_copy(
                            answer.at[pl.ds(pl.multiple_of((g * TRAINERS + to) * 8, 8), 8)],
                            weights.at[pl.ds(pl.multiple_of(column * 8, 8), 8)],
                            down_send,
                            down_recv,
                            device_id=device(g, to),
                        ).start()
                    return carry

                lax.fori_loop(0, TRAINERS, send, 0, unroll=True)
        own = delta.at[pl.ds(pl.multiple_of(column * 8, 8), 8)]
        part = running[OWNERS : OWNERS + 8] + summed(ones)
        own[...] = inner_rate * jnp.concatenate([part[:1, r * 128 : (r + 1) * 128] for r in range(8)], axis=0)

        def tell(j, carry):
            to = far_first(column, j)
            for g in (0, last_group):
                pltpu.make_async_remote_copy(own, own, last_send, last_recv, device_id=device(g, to)).start()
            return carry

        lax.fori_loop(0, TRAINERS - 1, tell, 0, unroll=True)
        pltpu.make_async_remote_copy(own, own, last_send, last_recv, device_id=device(0, column)).start()
        others = delta.at[pl.ds(0, (TILES - 1) * 8)]
        whole(answer, down_send).wait()
        whole(others, last_recv).wait()
        hand = pltpu.make_async_remote_copy(delta, delta, hand_send, last_recv, device_id={"grp": 2})
        hand.start()
        whole(delta, last_send).wait()
        whole(others, last_send).wait()
        hand.wait_send()
        keep.wait()

    values = delta[...]
    inverse = lax.rsqrt(jnp.sum(values * values) / NPARAM + norm_epsilon)
    table = jnp.where(me < CH, table_of(delta, 0), table_of(delta, 1))
    share[...] = inverse * share_of(table, share_pick, share_unit)


def step_call(sample_block, sample_trainer, closure_out, closure_in, closure_bias, master, brick):
    vmem = pl.BlockSpec(memory_space=pltpu.VMEM)
    hbm = pl.BlockSpec(memory_space=pltpu.HBM)
    dma = pltpu.SemaphoreType.DMA
    operands = (
        sample_block, sample_trainer, closure_out, closure_in.T, closure_bias.reshape(1, CH),
        sample_trainer.reshape(1, OWNERS), master.reshape(135, 128), brick,
    )
    operands = [pltpu.with_memory_space_constraint(x, pltpu.HBM) for x in operands]
    spaces = [pltpu.SMEM] * 3 + [pltpu.VMEM] * 4
    return pl.pallas_call(
        step_kernel,
        out_shape=(
            jax.ShapeDtypeStruct((F, CX, CY, CZ), f32),
            jax.ShapeDtypeStruct((1, 135), f32),
        ),
        in_specs=[hbm] * 8,
        out_specs=(vmem, vmem),
        scratch_shapes=[space(x.shape, x.dtype) for space, x in zip(spaces, operands)]
        + [
            pltpu.VMEM((1024, 256), bf16),
            pltpu.VMEM((F, CX + 2, CY, CZ), f32),
            pltpu.VMEM((F, CX, CZ), f32),
            pltpu.VMEM((F, CX, CZ), f32),
            pltpu.VMEM((2, F, CX, CZ), f32),
            pltpu.VMEM((16, CELLS), bf16),
            pltpu.VMEM((F, 18, 16, 128), f32),
            pltpu.VMEM((F, 16, 128), f32),
            pltpu.VMEM((F, 16, 128), f32),
            pltpu.VMEM((4, 16, 512), f32),
            pltpu.VMEM((2, F, 16, 128), f32),
            pltpu.VMEM((2, F, 16, 128), f32),
            pltpu.VMEM((2, F, 16, 128), f32),
            pltpu.VMEM((CX, 160, 128), bf16),
            pltpu.VMEM((160, CELLS), bf16),
            pltpu.VMEM((KROWS, WIDE), bf16),
            pltpu.VMEM((3 * CH, WIDE), bf16),
            pltpu.VMEM((CH, CELLS), f32),
            pltpu.VMEM((KROWS, WIDE), bf16),
            pltpu.VMEM((CH, CELLS), bf16),
            pltpu.VMEM((CH, KROWS), bf16),
            pltpu.VMEM((CH, KROWS), bf16),
            pltpu.VMEM((80, 3 * CH), bf16),
            pltpu.VMEM((TILES * 8, 128), f32),
            pltpu.VMEM((TILES * 8, 128), f32),
            pltpu.VMEM((TILES * 8, 128), f32),
            pltpu.VMEM((OWNERS * 8, 128), f32),
            pltpu.VMEM((OWNERS * 8, 128), f32),
            pltpu.VMEM((OWNERS + 8, 1024), f32),
            pltpu.VMEM((TILES * 8, 128), f32),
            pltpu.VMEM((144, 256), bf16),
            pltpu.VMEM((CH, 144), f32),
            dma((7,)),
            dma,
            dma((4,)),
            dma((4,)),
            dma((4,)),
            dma((4,)),
            dma,
            dma,
            dma,
            dma,
            dma,
            dma,
            dma,
        ],
        compiler_params=pltpu.CompilerParams(vmem_limit_bytes=50 * 2**20, has_side_effects=True, collective_id=0),
    )(*operands)


def finish_kernel(made, share, momentum, master, new_fields, new_master, new_momentum, in_sems, out_sems):
    out = [pltpu.make_async_copy(made.at[f], new_fields.at[f], out_sems.at[f]) for f in range(F)]
    columns = lax.axis_size("gy")
    me = lax.axis_index("grp") * TRAINERS + lax.axis_index("gx") * columns + lax.axis_index("gy")
    begin = me * 135
    row = begin // 128

    def mine(flat):
        rows = [flat[pl.ds(jnp.minimum(row + i, 134), 1), :] for i in range(3)]
        wide = jnp.broadcast_to(jnp.concatenate(rows, axis=1), (8, 384))
        return pltpu.roll(wide, lax.rem(384 - begin % 128, 384), 1)[:1, :135]

    momentum_share = momentum_decay * mine(momentum) + share[...]
    new_momentum[...] = momentum_share
    new_master[...] = mine(master) - outer_rate * momentum_share
    for f in range(F):
        out[f].start()
    for f in range(F):
        out[f].wait()


def finish_call(made, share, momentum, master):
    vmem = pl.BlockSpec(memory_space=pltpu.VMEM)
    hbm = pl.BlockSpec(memory_space=pltpu.HBM)
    part = jax.ShapeDtypeStruct((1, 135), f32)
    return pl.pallas_call(
        finish_kernel,
        out_shape=(jax.ShapeDtypeStruct(made.shape, made.dtype), part, part),
        in_specs=[vmem, vmem, vmem, vmem],
        out_specs=(hbm, vmem, vmem),
        scratch_shapes=[
            pltpu.SemaphoreType.DMA((F,)),
            pltpu.SemaphoreType.DMA((F,)),
        ],
        compiler_params=pltpu.CompilerParams(vmem_limit_bytes=6 * 2**20),
    )(made, share, momentum.reshape(135, 128), master.reshape(135, 128))


def on_device(
    fields, closure_in, closure_bias, closure_out, master, momentum, sample_block, sample_trainer
):
    made, share = step_call(
        sample_block, sample_trainer, closure_out, closure_in, closure_bias, master, fields[0]
    )
    new_fields, new_master, new_momentum = finish_call(made, share, momentum, master)
    return (new_fields[None], new_master.reshape(135), new_momentum.reshape(135))


def solution(mesh):
    in_specs = (P("grp", None, "gx", "gy", None), P(), P(), P(), P(), P(), P(), P())
    out_specs = (P("grp", None, "gx", "gy", None), P(("grp", "gx", "gy")), P(("grp", "gx", "gy")))
    return jax.shard_map(
        on_device, mesh=mesh, in_specs=in_specs, out_specs=out_specs, check_vma=False
    )
```
